128 devices in a mesh: wide: 32 (over x_hi, z, y), narrow: 4 (over x_lo, core).
Axes of the slice: x: 4 (x_hi: 2, x_lo: 2; x = x_hi * 2 + x_lo), y: 4, z: 4, core: 2. Of those that a mesh axis runs over, the one named last changes fastest.
Arguments:
- tokens: bfloat16 [3072, 4096], P('wide'), may hold values from -6 to 6
- expert_ids: int32 [3072, 8], P('wide'), may hold values from 0 to 63, all different within a row; in each aligned block of 96 rows (0 to 95, 96 to 191, ...) at most 16 rows name the same one
- probs: float32 [3072, 8], P('wide'), may hold values from 0.02 to 1
- w_in: bfloat16 [64, 2, 4096, 1536], P('wide', None, None, 'narrow'), may hold values from -0.09375 to 0.09375
- w_down: bfloat16 [64, 1536, 4096], P('wide', 'narrow'), may hold values from -0.15625 to 0.15625
- fresh_in: bfloat16 [2, 65536, 1536], P(None, 'wide', 'narrow'), may hold values from -0.09375 to 0.09375
- fresh_down: bfloat16 [1536, 65536], P('narrow', 'wide'), may hold values from -0.15625 to 0.15625
- refresh_slot: int32 [16], replicated, may hold values from 0 to 3, as said below
Outputs:
- mixed: bfloat16 [3072, 4096], P('wide', 'narrow')
The draws below stay inside these ranges and needn't reach their ends.
Inputs may be any that keep to these rules, and one draw needn't show every extreme that they name: `expert_ids`: in each block of 96 rows (the rows of one index of wide), no expert is named by more than 16 choices, a bound that some block reaches; a row names 8 different experts. refresh_slot[p] lies in (p mod 2) * 2 to (p mod 2) * 2 + 1, so pair p's refreshed expert is held by index 2 * p + (p mod 2) of wide; refresh_slot[0] is 0 and the last pair's is 3.
All inputs are finite; a program needn't handle non-finite values.
Results may differ from the reference program's by a relative error of at most 0.015.
Values may be sent and summed in bfloat16 or wider, within the bound.
A program may use at most 192 MiB of HBM per device.

```python
import math
import jax
import jax.numpy as jnp
import numpy as np
from jax import lax

D = 4096
FF = 1536
TOP = 8
EXP_DEV = 2
ROW_DEV = 96
EXPERTS = 64
CAP = 16
PAIRS = 16
ROWS = 3072
N_WIDE = 32
N_NARROW = 4


def draw_refresh_slot(key, part):
    key = jax.random.fold_in(key, 11)
    pair_ids = jnp.arange(PAIRS, dtype=jnp.int32)
    picked = jax.random.randint(key, (PAIRS,), 0, EXP_DEV, dtype=jnp.int32)
    picked = jnp.where(pair_ids == 0, jnp.zeros_like(picked), picked)
    picked = jnp.where(pair_ids == PAIRS - 1, jnp.full_like(picked, EXP_DEV - 1), picked)
    return pair_ids % 2 * EXP_DEV + picked


def level_of(own_key, extent, split, least, largest):
    def one(axis_at, blocks):
        steps = jax.random.uniform(jax.random.fold_in(jax.random.fold_in(own_key, 6), axis_at), (blocks,), jnp.float32, least / len(split), largest / len(split))
        return jnp.repeat(jnp.exp(steps), extent[axis_at] // blocks).reshape((-1,) + (1,) * (len(extent) - axis_at - 1))

    gain = one(*split[0])
    for cut in split[1:]:
        gain = gain * one(*cut)
    return gain


def deal_out(stream_key, own, number, rows, amount, top, bound, skew):
    ranking = jax.random.permutation(stream_key, amount)
    crowded, ordinary = load_shares(amount, rows * top, bound, skew, True), load_shares(amount, rows * top, bound, skew, False)
    places = jnp.arange(amount)

    def named(lengths, offset_by):
        used = int((lengths > 0).sum())
        fixed = max(1, used // 4)
        moved = fixed + (places - fixed + offset_by * (used - fixed)) % max(1, amount - fixed)
        return jnp.zeros((amount,), jnp.int32).at[ranking[jnp.where(places < fixed, places, moved)]].set(jnp.asarray(lengths, jnp.int32))

    lengths = jnp.where(number % 4 == 0, named(crowded, number // 4), named(ordinary, number - number // 4 - 1))
    mixed = jax.random.permutation(jax.random.fold_in(own, 3), amount)
    giver, taker = mixed[0:amount // 2 * 2:2], mixed[1:amount // 2 * 2:2]
    margin = jnp.minimum(lengths[giver] - 1, bound - lengths[taker]) // 2
    margin = jnp.where((giver == ranking[0]) | (taker == ranking[0]) | (lengths[taker] == 0), 0, jnp.maximum(margin, 0))
    moved = jax.random.randint(jax.random.fold_in(own, 4), (amount // 2,), 0, 1 << 20) % (margin + 1)
    lengths = lengths.at[giver].add(-moved).at[taker].add(moved)
    members = jnp.searchsorted(jnp.cumsum(lengths), jnp.arange(rows * top), side="right").astype(jnp.int32)
    table = members.reshape(top, rows).T
    table = table[jax.random.permutation(jax.random.fold_in(own, 1), rows)]
    offset_by = jax.random.randint(jax.random.fold_in(own, 2), (rows, 1), 0, top)
    return jnp.take_along_axis(table, (jnp.arange(top)[None, :] + offset_by) % top, axis=1)


def load_shares(amount, total, reach, slope, full):
    loads = [(1 << 20) // math.isqrt(standing ** slope) + 1 for standing in range(1, amount + 1)]
    largest = reach if full else min(reach, max(-(-total // amount), total * loads[0] // sum(loads)))
    least = 1 if total - largest >= amount - 1 else 0
    holding, rest = [largest] + [least] * (amount - 1), total - largest - least * (amount - 1)
    while rest > 0:
        free = [i for i in range(1, amount) if holding[i] < largest] or [i for i in range(1, amount) if holding[i] < reach]
        whole, budget = sum([loads[i] for i in free]), rest
        for i in free:
            extra = min(reach - holding[i], max(1, budget * loads[i] // whole), rest)
            holding[i] = holding[i] + extra
            rest = rest - extra
    return np.array(holding)


def noise(key, shape, scale, bound, shards=(), held_as=jnp.bfloat16):
    values = jax.random.normal(key, shape, jnp.float32) * scale
    if len(shards) > 0:
        values = level_of(key, shape, shards, -0.22, 0.18) * values
    return jnp.clip(values, min=-bound, max=bound).astype(held_as)


def setup_inputs(seed: int = 0) -> dict:
    key_of = jax.random.split(jax.random.key(seed), 9)
    tokens = noise(key_of[0], (ROWS, D), 1.0, 6.0, ((0, 32),))
    expert_ids_keys = jax.random.split(jax.random.fold_in(key_of[1], 1), ROWS // ROW_DEV)
    expert_ids_turns = jax.random.permutation(jax.random.fold_in(key_of[1], 3), ROWS // ROW_DEV)
    expert_ids = jax.vmap(lambda own, number: deal_out(jax.random.fold_in(key_of[1], 2), own, number, ROW_DEV, EXPERTS, TOP, CAP, 2))(expert_ids_keys, expert_ids_turns).reshape((ROWS, TOP))
    probs = jnp.clip(jnp.exp(math.log(1.0) - 3.912023 * jax.random.uniform(key_of[2], (ROWS, TOP), jnp.float32) ** level_of(key_of[2], (ROWS, TOP), ((0, 32),), -0.2, 0.2)), 0.02, 1.0)
    w_in = noise(key_of[3], (EXPERTS, 2, D, FF), D ** -0.5, 0.09375, ((0, 32), (3, 4)))
    w_down = noise(key_of[4], (EXPERTS, FF, D), FF ** -0.5, 0.15625, ((0, 32), (1, 4)))
    fresh_in = noise(key_of[5], (2, PAIRS * D, FF), D ** -0.5, 0.09375, ((1, 32), (2, 4)))
    fresh_down = noise(key_of[6], (FF, PAIRS * D), FF ** -0.5, 0.15625, ((0, 4), (1, 32)))
    refresh_slot = draw_refresh_slot(jax.random.fold_in(key_of[8], 71), 0)
    return {"tokens": tokens, "expert_ids": expert_ids, "probs": probs, "w_in": w_in, "w_down": w_down, "fresh_in": fresh_in, "fresh_down": fresh_down, "refresh_slot": refresh_slot}


def place(flat_ids, experts, capacity):
    entries = flat_ids.shape[0]
    onehot = (flat_ids[:, None] == jnp.arange(experts, dtype=jnp.int32)[None, :]).astype(jnp.int32)
    earlier = jnp.cumsum(onehot, axis=0) - onehot
    position = jnp.sum(earlier * onehot, axis=1)
    target = flat_ids * capacity + position
    source = jnp.zeros((experts * capacity,), jnp.int32).at[target].set(jnp.arange(entries, dtype=jnp.int32))
    filled = jnp.zeros((experts * capacity,), jnp.int32).at[target].set(jnp.ones((entries,), jnp.int32))
    return target, source, filled


def reference(tokens, expert_ids, probs, w_in, w_down, fresh_in, fresh_down, refresh_slot):
    parts = N_NARROW
    blockw = FF // parts
    sectioned = fresh_in.reshape(2, PAIRS, D, parts, blockw)
    sectioned = jnp.swapaxes(sectioned, 3, 4).reshape(2, PAIRS, D, FF)
    rolled_in = jnp.transpose(sectioned, (1, 0, 2, 3))
    lowered = fresh_down.reshape(parts, blockw, PAIRS, D)
    lowered = jnp.swapaxes(lowered, 0, 1).reshape(FF, PAIRS, D)
    rolled_down = jnp.transpose(lowered, (1, 0, 2))

    blocks = expert_ids.reshape(N_WIDE, ROW_DEV * TOP)
    targets, sources, fills = jax.vmap(lambda one: place(one, EXPERTS, CAP))(blocks)
    sources = jnp.transpose(sources.reshape(N_WIDE, EXPERTS, CAP), (1, 0, 2))
    fills = jnp.transpose(fills.reshape(N_WIDE, EXPERTS, CAP), (1, 0, 2))
    row_index = jnp.arange(N_WIDE, dtype=jnp.int32)[None, :, None] * ROW_DEV + sources // TOP

    def one_expert(packed):
        expert, rows_idx, fill = packed
        pair = expert // (2 * EXP_DEV)
        match = refresh_slot[pair] == expert % (2 * EXP_DEV)
        w_pair = jnp.where(match, rolled_in[pair], w_in[expert])
        w_out = jnp.where(match, rolled_down[pair], w_down[expert])
        gathered = tokens[rows_idx.reshape(-1)]
        gathered = jnp.where(fill.reshape(-1)[:, None] > 0, gathered, jnp.zeros_like(gathered))
        gate = jnp.dot(gathered, w_pair[0], preferred_element_type=jnp.float32)
        upward = jnp.dot(gathered, w_pair[1], preferred_element_type=jnp.float32)
        hidden = (jax.nn.silu(gate) * upward).astype(jnp.bfloat16)
        total = jnp.zeros((N_WIDE * CAP, D), jnp.float32)
        for piece in range(parts):
            term = jnp.dot(hidden[:, piece * blockw:(piece + 1) * blockw], w_out[piece * blockw:(piece + 1) * blockw], preferred_element_type=jnp.float32)
            total = total + lax.optimization_barrier(term.astype(jnp.bfloat16)).astype(jnp.float32)
        return total.astype(jnp.bfloat16).reshape(N_WIDE, CAP, D)

    outputs = lax.map(one_expert, (jnp.arange(EXPERTS, dtype=jnp.int32), row_index, fills))
    chosen = targets // CAP
    slots = targets % CAP
    block_ids = jnp.broadcast_to(jnp.arange(N_WIDE, dtype=jnp.int32)[:, None], targets.shape)
    values = outputs[chosen, block_ids, slots].reshape(ROWS, TOP, D)
    weights = probs / jnp.sum(probs, axis=1, keepdims=True)
    mixed = jnp.sum(weights[:, :, None] * values.astype(jnp.float32), axis=1)
    return mixed.astype(jnp.bfloat16)
```

```python
import functools

import jax
import jax.numpy as jnp
from jax import lax
from jax.experimental import pallas as pl
from jax.experimental.pallas import tpu as pltpu
from jax.sharding import PartitionSpec as P

MESH = pl.DeviceIdType.MESH
CAP = 16
BF16 = jnp.bfloat16
F32 = jnp.float32


def dot(a, b):
    return jnp.dot(a, b, preferred_element_type=F32)


def routing(ids, probs, slots, sel_ref, coef_ref):
    rows, top = ids.shape
    count = sel_ref.shape[1]
    experts = count // CAP
    pairs = experts // 4
    q = lax.broadcasted_iota(jnp.int32, (1, experts), 1)
    kind, pair = q // pairs, q % pairs
    fresh = jnp.zeros((1, experts), jnp.int32)
    for p in range(pairs):
        fresh = jnp.where(pair == p, slots[p], fresh)
    odd = pair % 2
    kept = 4 * pair + 2 - 2 * odd
    expert = jnp.where(
        kind < 2, kept + kind, jnp.where(kind == 2, 4 * pair + 4 * odd + 1 - fresh, 4 * pair + fresh)
    )
    names = jnp.zeros((rows, experts), F32)
    weight = jnp.zeros((rows, experts), F32)
    for k in range(top):
        hit = ids[:, k : k + 1] == expert
        names = jnp.where(hit, 1.0, names)
        weight = jnp.where(hit, probs[:, k : k + 1], weight)
    weight = weight / jnp.sum(probs, axis=1, keepdims=True)
    later = lax.broadcasted_iota(jnp.int32, (rows, rows), 0)
    earlier = lax.broadcasted_iota(jnp.int32, (rows, rows), 1)
    before = jnp.where(earlier < later, 1.0, 0.0).astype(BF16)
    position = dot(before, names.astype(BF16))
    key = jnp.where(names > 0.0, position, -1.0).astype(BF16)
    column = lax.broadcasted_iota(jnp.int32, (experts, count), 1)
    spread = jnp.where(
        column // CAP == lax.broadcasted_iota(jnp.int32, (experts, count), 0), 1.0, 0.0
    ).astype(BF16)
    slot = (lax.broadcasted_iota(jnp.int32, (rows, count), 1) % CAP).astype(F32)
    sel = jnp.where(dot(key, spread) == slot, 1.0, 0.0)
    sel_ref[...] = sel.astype(BF16)
    high = weight.astype(BF16)
    low = (weight - high.astype(F32)).astype(BF16)
    coef_ref[:rows] = (sel * dot(high, spread)).astype(BF16)
    coef_ref[rows:] = (sel * dot(low, spread)).astype(BF16)


def gated(gate, up):
    return (gate / (1.0 + jnp.exp(-gate)) * up).astype(BF16)


def kernel(
    nwide,
    tok_hbm,
    ids_ref,
    probs_ref,
    slot_ref,
    wi_hbm,
    wd_hbm,
    fi_hbm,
    fd_hbm,
    out_ref,
    tok,
    sel,
    coef,
    picked,
    recv_r,
    recv_k,
    wi,
    wd,
    fi,
    fd,
    acc,
    hid,
    hid_r,
    part_out,
    part_in,
    in_r,
    in_k,
    ret,
    mix_out,
    mix_in,
    load_sem,
    dsend,
    drecv,
    fsend,
    frecv,
    osend,
    orecv,
    psend,
    precv,
    rsend,
    rrecv,
):
    rows, wblk = out_ref.shape
    total = nwide * CAP
    half = total // 2
    npair = nwide // 2
    per_kind = npair * CAP
    tile = wblk // 2
    wide, narrow = lax.axis_index("wide"), lax.axis_index("narrow")
    x_hi = wide // (nwide // 2)
    x_lo, core = narrow // 2, narrow % 2
    pair, side = wide // 2, wide % 2
    pair_odd = pair % 2
    owner = 1 - (side + pair_odd) % 2
    sibling = (wide, x_lo * 2 + 1 - core)
    mate = (wide, (1 - x_lo) * 2 + core)
    partner = (pair * 2 + 1 - side, narrow)

    def peer(index):
        other = (x_lo + x_hi + index // (nwide // 2)) % 2
        return (index, other * 2 + core)

    def remote(src, dst, send, recv, device):
        return pltpu.make_async_remote_copy(
            src_ref=src, dst_ref=dst, send_sem=send, recv_sem=recv, device_id=device, device_id_type=MESH
        )

    def arrived(ref, sem):
        pltpu.make_async_copy(ref, ref, sem).wait()

    def block(ref, index):
        return ref.at[pl.ds(pl.multiple_of(index * CAP, CAP), CAP)]

    loads = [
        pltpu.make_async_copy(
            tok_hbm.at[:, pl.ds(pl.multiple_of(core * wblk, wblk), wblk)], tok.at[:, :wblk], load_sem.at[0]
        ),
        pltpu.make_async_copy(
            tok_hbm.at[:, pl.ds(pl.multiple_of((core + 2) * wblk, wblk), wblk)],
            tok.at[:, wblk:],
            load_sem.at[1],
        ),
        pltpu.make_async_copy(fi_hbm, fi, load_sem.at[2]),
        pltpu.make_async_copy(fd_hbm, fd, load_sem.at[3]),
        pltpu.make_async_copy(wi_hbm, wi, load_sem.at[4]),
        pltpu.make_async_copy(wd_hbm, wd, load_sem.at[5]),
    ]
    for load in loads:
        load.start()

    barrier = pltpu.get_barrier_semaphore()

    def greet(i, carry):
        pl.semaphore_signal(
            barrier, inc=1, device_id=peer((wide + i) % nwide), device_id_type=MESH
        )
        return carry

    lax.fori_loop(1, nwide, greet, 0)
    pl.semaphore_signal(barrier, inc=1, device_id=sibling, device_id_type=MESH)
    pl.semaphore_signal(barrier, inc=1, device_id=mate, device_id_type=MESH)

    routing(ids_ref[...], probs_ref[...], slot_ref, sel, coef)
    loads[0].wait()
    loads[1].wait()

    def pick(kind):
        span = pl.ds(kind * per_kind, per_kind)
        picked[span, :] = lax.dot_general(
            sel[:, span], tok[...], (((0,), (0,)), ((), ())), preferred_element_type=F32
        ).astype(BF16)

    pick(3)
    pl.semaphore_wait(barrier, nwide + 1)

    def piece_r(index):
        return picked.at[
            pl.ds(pl.multiple_of(3 * per_kind + index // 2 * CAP, CAP), CAP),
            pl.ds(pl.multiple_of(index % 2 * wblk, wblk), wblk),
        ]

    def send_r(i, carry):
        index = (wide + i) % nwide
        remote(
            piece_r(index), block(recv_r.at[core], wide), dsend.at[2], drecv.at[2], peer(index)
        ).start()
        return carry

    lax.fori_loop(1, nwide, send_r, 0)
    pltpu.make_async_copy(piece_r(wide), block(recv_r.at[core], wide), drecv.at[2]).start()

    pick(0)
    pick(2)

    def piece_0(index):
        to_owner = 1 - (index % 2 + index // 2) % 2
        return picked.at[
            pl.ds(pl.multiple_of(to_owner * (2 * per_kind) + index // 2 * CAP, CAP), CAP)
        ]

    def send_0(i, carry):
        index = (wide + i) % nwide
        remote(
            piece_0(index), block(recv_k.at[0, core], wide), dsend.at[0], drecv.at[0], peer(index)
        ).start()
        return carry

    lax.fori_loop(1, nwide, send_0, 0)
    pltpu.make_async_copy(piece_0(wide), block(recv_k.at[0, core], wide), drecv.at[0]).start()

    pick(1)

    def piece_1(index):
        return picked.at[pl.ds(pl.multiple_of(per_kind + index * CAP, CAP), CAP)]

    def send_1(i, carry):
        to_pair = (pair + i) % npair
        index = 2 * to_pair + 1 - to_pair % 2

        @pl.when(index != wide)
        def _():
            remote(
                piece_1(to_pair),
                block(recv_k.at[1, core], wide),
                dsend.at[1],
                drecv.at[1],
                peer(index),
            ).start()

        return carry

    lax.fori_loop(0, npair, send_1, 0)

    @pl.when(owner == 0)
    def _():
        pltpu.make_async_copy(piece_1(pair), block(recv_k.at[1, core], wide), drecv.at[1]).start()

    mine = pl.ds(pl.multiple_of(side * half, half), half)
    theirs = pl.ds(pl.multiple_of((1 - side) * half, half), half)
    arrived(recv_r.at[core], drecv.at[2])
    forward = remote(recv_r.at[core], recv_r.at[core], fsend.at[2], frecv.at[2], sibling)
    forward.start()
    loads[2].wait()
    depth = pl.ds(pl.multiple_of(core * wblk, wblk), wblk)
    for g in range(2):
        acc[g] = dot(recv_r[core], fi[g, depth, :])
    arrived(recv_r.at[1 - core], frecv.at[2])
    depth = pl.ds(pl.multiple_of((1 - core) * wblk, wblk), wblk)
    for g in range(2):
        acc[g] += dot(recv_r[1 - core], fi[g, depth, :])
    for g in range(2):
        part_out[g] = acc[g, theirs, :].astype(BF16)
    swap = remote(part_out, part_in, psend.at[0], precv.at[0], partner)
    swap.start()
    loads[3].wait()
    swap.wait_recv()
    hid_r[mine, :] = gated(
        acc[0, mine, :] + part_in[0].astype(F32), acc[1, mine, :] + part_in[1].astype(F32)
    )
    share = remote(hid_r.at[mine], hid_r.at[mine], psend.at[1], precv.at[1], partner)
    share.start()
    forward.wait_send()
    arrived(hid_r.at[theirs], precv.at[1])
    given = []
    for t in range(2):
        span = pl.ds(t * tile, tile)
        columns = pl.ds(pl.multiple_of((1 - core) * wblk + t * tile, tile), tile)
        recv_r[1 - core, :, span] = dot(hid_r[...], fd[:, columns]).astype(BF16)
        copy = remote(
            recv_r.at[1 - core, :, span], in_r.at[:, span], osend.at[2, t], orecv.at[2, t], sibling
        )
        copy.start()
        given.append(copy)
    for t in range(2):
        span = pl.ds(t * tile, tile)
        columns = pl.ds(pl.multiple_of(core * wblk + t * tile, tile), tile)
        given[t].wait_recv()
        recv_r[core, :, span] = (
            dot(hid_r[...], fd[:, columns]) + in_r[:, span].astype(F32)
        ).astype(BF16)

    def slot_r():
        return ret.at[
            pl.ds(pl.multiple_of(3 * per_kind + pair * CAP, CAP), CAP),
            pl.ds(pl.multiple_of(side * wblk, wblk), wblk),
        ]

    def back_r(i, carry):
        index = (wide + i) % nwide
        remote(
            block(recv_r.at[core], index), slot_r(), rsend.at[2], rrecv.at[3], peer(index)
        ).start()
        return carry

    lax.fori_loop(1, nwide, back_r, 0)
    pltpu.make_async_copy(block(recv_r.at[core], wide), slot_r(), rrecv.at[3]).start()

    loads[4].wait()
    loads[5].wait()
    unchanged = (slot_ref[pair] + 1) % 2

    def one_expert(i, carry):
        expert = jnp.where(owner == 1, unchanged, i)
        kind = owner * 2 + (1 - owner) * i
        arrived(recv_k.at[i, core], drecv.at[i])
        forward = remote(recv_k.at[i, core], recv_k.at[i, core], fsend.at[i], frecv.at[i], sibling)
        forward.start()
        for b in range(2):
            depth = pl.ds(pl.multiple_of((core + 2 * b) * wblk, wblk), wblk)
            for g in range(2):
                part = dot(recv_k[i, core, :, b * wblk : (b + 1) * wblk], wi[expert, g, depth, :])
                if b == 0:
                    acc[g] = part
                else:
                    acc[g] += part
        arrived(recv_k.at[i, 1 - core], frecv.at[i])
        for b in range(2):
            depth = pl.ds(pl.multiple_of((1 - core + 2 * b) * wblk, wblk), wblk)
            for g in range(2):
                acc[g] += dot(
                    recv_k[i, 1 - core, :, b * wblk : (b + 1) * wblk], wi[expert, g, depth, :]
                )
        hid[...] = gated(acc[0], acc[1])
        forward.wait_send()
        given = []
        for t in range(4):
            span = pl.ds(t * tile, tile)
            first = (1 - core + t // 2 * 2) * wblk + t % 2 * tile
            columns = pl.ds(pl.multiple_of(first, tile), tile)
            recv_k[i, 1 - core, :, span] = dot(hid[...], wd[expert, :, columns]).astype(BF16)
            copy = remote(
                recv_k.at[i, 1 - core, :, span],
                in_k.at[i, :, span],
                osend.at[i, t],
                orecv.at[i, t],
                sibling,
            )
            copy.start()
            given.append(copy)
        for t in range(4):
            span = pl.ds(t * tile, tile)
            first = (core + t // 2 * 2) * wblk + t % 2 * tile
            columns = pl.ds(pl.multiple_of(first, tile), tile)
            given[t].wait_recv()
            recv_k[i, core, :, span] = (
                dot(hid[...], wd[expert, :, columns]) + in_k[i, :, span].astype(F32)
            ).astype(BF16)

        slot = ret.at[pl.ds(pl.multiple_of(kind * per_kind + pair * CAP, CAP), CAP)]

        def back(j, inner):
            index = (wide + j) % nwide
            remote(
                block(recv_k.at[i, core], index), slot, rsend.at[i], rrecv.at[kind], peer(index)
            ).start()
            return inner

        lax.fori_loop(1, nwide, back, 0)
        pltpu.make_async_copy(block(recv_k.at[i, core], wide), slot, rrecv.at[kind]).start()
        for t in range(4):
            given[t].wait_send()
        return carry

    lax.fori_loop(0, 2 - owner, one_expert, 0)

    for kind in (3, 0, 2, 1):
        arrived(ret.at[pl.ds(kind * per_kind, per_kind)], rrecv.at[kind])

    def mixed(which):
        both = dot(coef[...], ret[:, pl.ds(pl.multiple_of(which * wblk, wblk), wblk)])
        return both[:rows] + both[rows:]

    mix_out[...] = mixed(1 - x_lo).astype(BF16)
    last = remote(mix_out, mix_in, psend.at[2], precv.at[2], mate)
    last.start()
    own = mixed(x_lo)
    last.wait_recv()
    out_ref[...] = (own + mix_in[...].astype(F32)).astype(BF16)

    swap.wait_send()
    share.wait_send()
    last.wait_send()
    for copy in given:
        copy.wait_send()
    sent = total - CAP
    arrived(recv_r.at[0, pl.ds(0, sent)], dsend.at[2])
    arrived(recv_r.at[0, pl.ds(0, sent)], rsend.at[2])
    arrived(recv_k.at[0, 0, pl.ds(0, sent)], dsend.at[0])
    arrived(recv_k.at[0, 0, pl.ds(0, sent)], rsend.at[0])

    @pl.when(owner == 1)
    def _():
        arrived(recv_k.at[0, 0, pl.ds(0, per_kind)], dsend.at[1])

    @pl.when(owner == 0)
    def _():
        arrived(recv_k.at[0, 0, pl.ds(0, per_kind - CAP)], dsend.at[1])
        arrived(recv_k.at[0, 0, pl.ds(0, sent)], rsend.at[1])


def on_device(nwide, tokens, expert_ids, probs, w_in, w_down, fresh_in, fresh_down, refresh_slot):
    rows, width = tokens.shape
    units = w_down.shape[1]
    wblk = width // 4
    total = nwide * CAP
    slots = 2 * total
    dma = pltpu.SemaphoreType.DMA
    hbm = pl.BlockSpec(memory_space=pl.ANY)
    vmem = pl.BlockSpec(memory_space=pltpu.VMEM)
    return pl.pallas_call(
        functools.partial(kernel, nwide),
        out_shape=jax.ShapeDtypeStruct((rows, wblk), BF16),
        in_specs=[hbm, vmem, vmem, pl.BlockSpec(memory_space=pltpu.SMEM), hbm, hbm, hbm, hbm],
        out_specs=vmem,
        scratch_shapes=[
            pltpu.VMEM((rows, 2 * wblk), BF16),
            pltpu.VMEM((rows, slots), BF16),
            pltpu.VMEM((2 * rows, slots), BF16),
            pltpu.VMEM((slots, 2 * wblk), BF16),
            pltpu.VMEM((2, total, wblk), BF16),
            pltpu.VMEM((2, 2, total, 2 * wblk), BF16),
            pltpu.VMEM(w_in.shape, BF16),
            pltpu.VMEM(w_down.shape, BF16),
            pltpu.VMEM(fresh_in.shape, BF16),
            pltpu.VMEM(fresh_down.shape, BF16),
            pltpu.VMEM((2, total, units), F32),
            pltpu.VMEM((total, units), BF16),
            pltpu.VMEM((total, units), BF16),
            pltpu.VMEM((2, total // 2, units), BF16),
            pltpu.VMEM((2, total // 2, units), BF16),
            pltpu.VMEM((total, wblk), BF16),
            pltpu.VMEM((2, total, 2 * wblk), BF16),
            pltpu.VMEM((slots, 2 * wblk), BF16),
            pltpu.VMEM((rows, wblk), BF16),
            pltpu.VMEM((rows, wblk), BF16),
            dma((6,)),
            dma((3,)),
            dma((3,)),
            dma((3,)),
            dma((3,)),
            dma((3, 4)),
            dma((3, 4)),
            dma((3,)),
            dma((3,)),
            dma((3,)),
            dma((4,)),
        ],
        compiler_params=pltpu.CompilerParams(
            collective_id=0, has_side_effects=True, vmem_limit_bytes=63 * 1024 * 1024
        ),
    )(tokens, expert_ids, probs, refresh_slot, w_in, w_down, fresh_in, fresh_down)


def solution(mesh):
    return jax.shard_map(
        functools.partial(on_device, mesh.shape["wide"]),
        mesh=mesh,
        in_specs=(
            P("wide", None),
            P("wide", None),
            P("wide", None),
            P("wide", None, None, "narrow"),
            P("wide", "narrow", None),
            P(None, "wide", "narrow"),
            P("narrow", "wide"),
            P(),
        ),
        out_specs=P("wide", "narrow"),
        check_vma=False,
    )
```

```python
import functools

import jax
import jax.numpy as jnp
from jax import lax
from jax.experimental import pallas as pl
from jax.experimental.pallas import tpu as pltpu
from jax.sharding import PartitionSpec as P

MESH = pl.DeviceIdType.MESH
CAP = 16
GROUPS = 4
BF16 = jnp.bfloat16
F32 = jnp.float32


def dot(a, b):
    return jnp.dot(a, b, preferred_element_type=F32)


def routing(ids, probs, slots):
    top, rows = ids.shape
    pairs = slots.shape[0]
    experts = 4 * pairs
    q = lax.broadcasted_iota(jnp.int32, (experts, 1), 0)
    kind, pair = q // pairs, q % pairs
    fresh = jnp.zeros((experts, 1), jnp.int32)
    for p in range(pairs):
        fresh = jnp.where(pair == p, slots[p], fresh)
    odd = pair % 2
    kept = 4 * pair + 2 - 2 * odd
    expert = jnp.where(
        kind < 2, kept + kind, jnp.where(kind == 2, 4 * pair + 4 * odd + 1 - fresh, 4 * pair + fresh)
    )
    names = jnp.zeros((experts, rows), F32)
    weight = jnp.zeros((experts, rows), F32)
    for k in range(top):
        hit = ids[k : k + 1] == expert
        names = jnp.where(hit, 1.0, names)
        weight = jnp.where(hit, probs[k : k + 1], weight)
    weight = weight / jnp.sum(probs, axis=0, keepdims=True)
    earlier = lax.broadcasted_iota(jnp.int32, (rows, rows), 0)
    later = lax.broadcasted_iota(jnp.int32, (rows, rows), 1)
    before = jnp.where(earlier < later, 1.0, 0.0).astype(BF16)
    position = dot(names.astype(BF16), before)
    return jnp.where(names > 0.0, position, -1.0).astype(BF16), weight


def spread(kind, pairs):
    row = lax.broadcasted_iota(jnp.int32, (pairs * CAP, 4 * pairs), 0)
    column = lax.broadcasted_iota(jnp.int32, (pairs * CAP, 4 * pairs), 1)
    return jnp.where(row // CAP + kind * pairs == column, 1.0, 0.0).astype(BF16)


def gated(gate, up):
    return (gate / (1.0 + jnp.exp(-gate)) * up).astype(BF16)


def kernel(
    nwide,
    tok_hbm,
    ids_ref,
    probs_ref,
    slot_ref,
    wi_hbm,
    wd_hbm,
    fi_hbm,
    fd_hbm,
    out_ref,
    tok,
    sel,
    coef,
    picked,
    recv_r,
    recv_k,
    wi,
    wd,
    fi,
    fd,
    acc,
    hid,
    hid_r,
    part_out,
    part_in,
    part_own,
    in_r,
    in_k,
    ret,
    mix_out,
    mix_in,
    load_sem,
    dsend,
    drecv,
    fsend,
    frecv,
    csend,
    crecv,
    osend,
    orecv,
    psend,
    precv,
    rsend,
    rrecv,
):
    rows, wblk = out_ref.shape
    total = nwide * CAP
    half = total // 2
    npair = nwide // 2
    per_kind = npair * CAP
    tile = wblk // 2
    lone = 3 * wblk // 4
    direct = 2 * wblk - lone
    common = wblk - lone
    group = nwide // GROUPS
    span_g = group * CAP
    wide, narrow = lax.axis_index("wide"), lax.axis_index("narrow")
    x_hi = wide // (nwide // 2)
    x_lo, core = narrow // 2, narrow % 2
    pair, side = wide // 2, wide % 2
    pair_odd = pair % 2
    owner = 1 - (side + pair_odd) % 2
    sibling = (wide, x_lo * 2 + 1 - core)
    mate = (wide, (1 - x_lo) * 2 + core)
    partner = (pair * 2 + 1 - side, narrow)

    def peer(index):
        other = (x_lo + x_hi + index // (nwide // 2)) % 2
        return (index, other * 2 + core)

    def turn(i, sign=1):
        plane, step = nwide // 2, i // 2
        if plane == 16:
            z = wide // 4 % 4 + 4 + sign * ((step + step // 4) % 4)
            y = wide % 4 + 4 + sign * (step % 4)
            spot = z % 4 * 4 + y % 4
        else:
            spot = (wide + plane + sign * step) % plane
        return (x_hi + i) % 2 * plane + spot

    def remote(src, dst, send, recv, device):
        return pltpu.make_async_remote_copy(
            src_ref=src, dst_ref=dst, send_sem=send, recv_sem=recv, device_id=device, device_id_type=MESH
        )

    def arrived(ref, sem):
        pltpu.make_async_copy(ref, ref, sem).wait()

    def across(which):
        return pl.ds(pl.multiple_of(which * lone, 128), direct)

    def alone(which):
        return pl.ds(pl.multiple_of(which * direct, 128), lone)

    def block(ref, index):
        return ref.at[pl.ds(pl.multiple_of(index * CAP, CAP), CAP)]

    loads = [
        pltpu.make_async_copy(
            tok_hbm.at[:, pl.ds(pl.multiple_of(core * wblk, wblk), wblk)], tok.at[:, :wblk], load_sem.at[0]
        ),
        pltpu.make_async_copy(
            tok_hbm.at[:, pl.ds(pl.multiple_of((core + 2) * wblk, wblk), wblk)],
            tok.at[:, wblk:],
            load_sem.at[1],
        ),
        pltpu.make_async_copy(fi_hbm, fi, load_sem.at[2]),
        pltpu.make_async_copy(fd_hbm, fd, load_sem.at[3]),
        pltpu.make_async_copy(wi_hbm, wi, load_sem.at[4]),
        pltpu.make_async_copy(wd_hbm, wd, load_sem.at[5]),
    ]
    for load in loads:
        load.start()

    barrier = pltpu.get_barrier_semaphore()

    def greet(i, carry):
        pl.semaphore_signal(
            barrier, inc=1, device_id=peer(turn(i)), device_id_type=MESH
        )
        return carry

    lax.fori_loop(1, nwide, greet, 0)
    pl.semaphore_signal(barrier, inc=1, device_id=sibling, device_id_type=MESH)
    pl.semaphore_signal(barrier, inc=1, device_id=mate, device_id_type=MESH)

    key, weight = routing(ids_ref[...], probs_ref[...], slot_ref)
    loads[0].wait()
    loads[1].wait()

    def pick(kind):
        span = pl.ds(kind * per_kind, per_kind)
        slot = lax.broadcasted_iota(jnp.int32, (per_kind, rows), 0) % CAP
        chosen = jnp.where(dot(spread(kind, npair), key) == slot.astype(F32), 1.0, 0.0).astype(BF16)
        sel[span, :] = chosen
        picked[span, :] = dot(chosen, tok[...]).astype(BF16)

    pick(3)
    pl.semaphore_wait(barrier, nwide + 1)

    def piece_r(index):
        return picked.at[
            pl.ds(pl.multiple_of(3 * per_kind + index // 2 * CAP, CAP), CAP),
            pl.ds(pl.multiple_of(index % 2 * wblk, wblk), wblk),
        ]

    def send_r(i, carry):
        index = turn(i)
        remote(
            piece_r(index), block(recv_r.at[core], wide), dsend.at[2], drecv.at[2, 0], peer(index)
        ).start()
        return carry

    lax.fori_loop(1, nwide, send_r, 0)
    pltpu.make_async_copy(piece_r(wide), block(recv_r.at[core], wide), drecv.at[2, 0]).start()

    pick(0)
    pick(2)

    def send_kept(i, which, row):
        index = turn(i)
        device = peer(index)
        columns = across(device[1] // 2)
        remote(
            picked.at[pl.ds(pl.multiple_of(row(index), CAP), CAP), columns],
            block(recv_k.at[which, core], i).at[:, columns],
            dsend.at[which],
            drecv.at[which, i // group],
            device,
        ).start()

    def keep_kept(which, row):
        columns = across(x_lo)
        pltpu.make_async_copy(
            picked.at[pl.ds(pl.multiple_of(row(wide), CAP), CAP), columns],
            block(recv_k.at[which, core], 0).at[:, columns],
            drecv.at[which, 0],
        ).start()

    def row_0(index):
        to_owner = 1 - (index % 2 + index // 2) % 2
        return to_owner * (2 * per_kind) + index // 2 * CAP

    def send_0(i, carry):
        send_kept(i, 0, row_0)
        return carry

    lax.fori_loop(1, nwide, send_0, 0)
    keep_kept(0, row_0)

    pick(1)

    def row_1(index):
        return per_kind + index // 2 * CAP

    def send_1(i, carry):
        index = turn(i)

        @pl.when((index % 2 + index // 2) % 2 == 1)
        def _():
            send_kept(i, 1, row_1)

        return carry

    lax.fori_loop(1, nwide, send_1, 0)

    @pl.when(owner == 0)
    def _():
        keep_kept(1, row_1)

    high = weight.astype(BF16)
    low = (weight - high.astype(F32)).astype(BF16)
    for part, value in enumerate((high, low)):
        for kind in range(4):
            span = pl.ds(kind * per_kind, per_kind)
            taken = sel[span, :].astype(F32) * dot(spread(kind, npair), value)
            coef[part * rows : (part + 1) * rows, span] = taken.T.astype(BF16)

    mine = pl.ds(pl.multiple_of(side * half, half), half)
    theirs = pl.ds(pl.multiple_of((1 - side) * half, half), half)
    forward = remote(recv_r.at[core], recv_r.at[core], fsend.at[2, 0, 0], frecv.at[2, 0, 0], sibling)
    swap = remote(part_out, part_in, psend.at[0], precv.at[0], partner)
    share = remote(hid_r.at[mine], hid_r.at[mine], psend.at[1], precv.at[1], partner)

    def fresh_partial():
        arrived(recv_r.at[core], drecv.at[2, 0])
        forward.start()
        loads[2].wait()
        depth = pl.ds(pl.multiple_of(core * wblk, wblk), wblk)
        for g in range(2):
            acc[g] = dot(recv_r[core], fi[g, depth, :])
        forward.wait_recv()
        depth = pl.ds(pl.multiple_of((1 - core) * wblk, wblk), wblk)
        for g in range(2):
            acc[g] += dot(recv_r[1 - core], fi[g, depth, :])
        for g in range(2):
            part_out[g] = acc[g, theirs, :].astype(BF16)
            part_own[g] = acc[g, mine, :]
        swap.start()

    def fresh_hidden():
        swap.wait_recv()
        hid_r[mine, :] = gated(
            part_own[0] + part_in[0].astype(F32), part_own[1] + part_in[1].astype(F32)
        )
        share.start()

    def give(which, t, source, target, span):
        return remote(
            source.at[:, span], target.at[:, span], osend.at[which, t], orecv.at[which, t], sibling
        )

    def fresh_down_and_back():
        loads[3].wait()
        forward.wait_send()
        arrived(hid_r.at[theirs], precv.at[1])
        given = []
        for t in range(2):
            span = pl.ds(t * tile, tile)
            columns = pl.ds(pl.multiple_of((1 - core) * wblk + t * tile, tile), tile)
            recv_r[1 - core, :, span] = dot(hid_r[...], fd[:, columns]).astype(BF16)
            given.append(give(2, t, recv_r.at[1 - core], in_r, span))
            given[t].start()
        for t in range(2):
            span = pl.ds(t * tile, tile)
            columns = pl.ds(pl.multiple_of(core * wblk + t * tile, tile), tile)
            given[t].wait_recv()
            recv_r[core, :, span] = (
                dot(hid_r[...], fd[:, columns]) + in_r[:, span].astype(F32)
            ).astype(BF16)
        slot = ret.at[
            pl.ds(pl.multiple_of(3 * per_kind + pair * CAP, CAP), CAP),
            pl.ds(pl.multiple_of(side * wblk, wblk), wblk),
        ]

        def back(i, carry):
            index = turn(i)
            remote(
                block(recv_r.at[core], index), slot, rsend.at[2], rrecv.at[3], peer(index)
            ).start()
            return carry

        lax.fori_loop(1, nwide, back, 0)
        pltpu.make_async_copy(block(recv_r.at[core], wide), slot, rrecv.at[3]).start()
        for copy in given:
            copy.wait_send()

    unchanged = (slot_ref[pair] + 1) % 2
    near, far = across(x_lo), alone(1 - x_lo)

    def rows_of(which, g, columns, where=core):
        return recv_k.at[which, where, pl.ds(g * span_g, span_g), columns]

    def forward_near(which, g):
        ref = rows_of(which, g, near)
        return remote(ref, ref, fsend.at[which, g, 0], frecv.at[which, g, 0], sibling)

    def forward_far(which, g):
        ref = rows_of(which, g, far)
        return remote(ref, ref, fsend.at[which, g, 1], frecv.at[which, g, 1], sibling)

    def lend(which, g):
        ref = rows_of(which, g, alone(x_lo))
        return remote(ref, ref, csend.at[which, g], crecv.at[which, g], mate)

    def relay(which, g):
        if g < GROUPS:
            arrived(rows_of(which, g, near), drecv.at[which, g])
            lend(which, g).start()
            forward_near(which, g).start()
        if g > 0:
            arrived(rows_of(which, g - 1, far), crecv.at[which, g - 1])
            forward_far(which, g - 1).start()

    def gate_and_up(which, expert):
        def multiply(where, offset, row, size, first=False):
            offset, row = pl.multiple_of(offset, 128), pl.multiple_of(row, 128)
            for g in range(2):
                part = dot(
                    recv_k[which, where, :, pl.ds(offset, size)], wi[expert, g, pl.ds(row, size), :]
                )
                if first:
                    acc[g] = part
                else:
                    acc[g] += part

        def multiply_alone(where, chip, first=False):
            row = (where + 2 * chip) * wblk + chip * common
            multiply(where, chip * direct, row, lone, first)

        def multiply_common(where):
            multiply(where, lone, where * wblk + lone, common)
            multiply(where, wblk, (where + 2) * wblk, common)

        multiply_alone(core, x_lo, True)
        multiply_common(core)
        multiply_alone(core, 1 - x_lo)
        for g in range(GROUPS):
            forward_near(which, g).wait_recv()
        multiply_alone(1 - core, x_lo)
        multiply_common(1 - core)
        for g in range(GROUPS):
            forward_far(which, g).wait_recv()
        multiply_alone(1 - core, 1 - x_lo)
        hid[...] = gated(acc[0], acc[1])

    def down_and_back(which, expert, kind):
        for g in range(GROUPS):
            lend(which, g).wait_send()
            forward_near(which, g).wait_send()
            forward_far(which, g).wait_send()
        given = []
        for t in range(4):
            span = pl.ds(t * tile, tile)
            first = (1 - core + t // 2 * 2) * wblk + t % 2 * tile
            columns = pl.ds(pl.multiple_of(first, tile), tile)
            recv_k[which, 1 - core, :, span] = dot(hid[...], wd[expert, :, columns]).astype(BF16)
            given.append(give(which, t, recv_k.at[which, 1 - core], in_k.at[which], span))
            given[t].start()
        for t in range(4):
            span = pl.ds(t * tile, tile)
            first = (core + t // 2 * 2) * wblk + t % 2 * tile
            columns = pl.ds(pl.multiple_of(first, tile), tile)
            given[t].wait_recv()
            recv_k[which, core, :, span] = (
                dot(hid[...], wd[expert, :, columns]) + in_k[which, :, span].astype(F32)
            ).astype(BF16)
        slot = ret.at[pl.ds(pl.multiple_of(kind * per_kind + pair * CAP, CAP), CAP)]

        def back(i, carry):
            remote(
                block(recv_k.at[which, core], i),
                slot,
                rsend.at[which],
                rrecv.at[kind],
                peer(turn(i, -1)),
            ).start()
            return carry

        lax.fori_loop(1, nwide, back, 0)
        pltpu.make_async_copy(block(recv_k.at[which, core], 0), slot, rrecv.at[kind]).start()
        for copy in given:
            copy.wait_send()

    first_expert = owner * unchanged
    fresh_partial()
    for g in range(GROUPS + 1):
        relay(0, g)
    loads[4].wait()
    loads[5].wait()
    gate_and_up(0, first_expert)
    fresh_hidden()

    @pl.when(owner == 0)
    def _():
        relay(1, 0)

    down_and_back(0, first_expert, owner * 2)

    @pl.when(owner == 0)
    def _():
        relay(1, 1)
        relay(1, 2)

    fresh_down_and_back()

    @pl.when(owner == 0)
    def _():
        for g in range(3, GROUPS + 1):
            relay(1, g)
        gate_and_up(1, 1)
        down_and_back(1, 1, 1)

    for kind in (0, 2, 3, 1):
        arrived(ret.at[pl.ds(kind * per_kind, per_kind)], rrecv.at[kind])

    def mixed(which):
        both = dot(coef[...], ret[:, pl.ds(pl.multiple_of(which * wblk, wblk), wblk)])
        return both[:rows] + both[rows:]

    mix_out[...] = mixed(1 - x_lo).astype(BF16)
    last = remote(mix_out, mix_in, psend.at[2], precv.at[2], mate)
    last.start()
    own = mixed(x_lo)
    last.wait_recv()
    out_ref[...] = (own + mix_in[...].astype(F32)).astype(BF16)

    swap.wait_send()
    share.wait_send()
    last.wait_send()
    sent = total - CAP
    arrived(recv_r.at[0, pl.ds(0, sent)], dsend.at[2])
    arrived(recv_r.at[0, pl.ds(0, sent)], rsend.at[2])
    arrived(recv_k.at[0, 0, pl.ds(0, sent), :direct], dsend.at[0])
    arrived(recv_k.at[0, 0, pl.ds(0, sent)], rsend.at[0])

    @pl.when(owner == 1)
    def _():
        arrived(recv_k.at[0, 0, pl.ds(0, per_kind), :direct], dsend.at[1])

    @pl.when(owner == 0)
    def _():
        arrived(recv_k.at[0, 0, pl.ds(0, per_kind - CAP), :direct], dsend.at[1])
        arrived(recv_k.at[0, 0, pl.ds(0, sent)], rsend.at[1])


def on_device(nwide, tokens, expert_ids, probs, w_in, w_down, fresh_in, fresh_down, refresh_slot):
    rows, width = tokens.shape
    units = w_down.shape[1]
    wblk = width // 4
    total = nwide * CAP
    slots = 2 * total
    dma = pltpu.SemaphoreType.DMA
    hbm = pl.BlockSpec(memory_space=pl.ANY)
    vmem = pl.BlockSpec(memory_space=pltpu.VMEM)
    return pl.pallas_call(
        functools.partial(kernel, nwide),
        out_shape=jax.ShapeDtypeStruct((rows, wblk), BF16),
        in_specs=[hbm, vmem, vmem, pl.BlockSpec(memory_space=pltpu.SMEM), hbm, hbm, hbm, hbm],
        out_specs=vmem,
        scratch_shapes=[
            pltpu.VMEM((rows, 2 * wblk), BF16),
            pltpu.VMEM((slots, rows), BF16),
            pltpu.VMEM((2 * rows, slots), BF16),
            pltpu.VMEM((slots, 2 * wblk), BF16),
            pltpu.VMEM((2, total, wblk), BF16),
            pltpu.VMEM((2, 2, total, 2 * wblk), BF16),
            pltpu.VMEM(w_in.shape, BF16),
            pltpu.VMEM(w_down.shape, BF16),
            pltpu.VMEM(fresh_in.shape, BF16),
            pltpu.VMEM(fresh_down.shape, BF16),
            pltpu.VMEM((2, total, units), F32),
            pltpu.VMEM((total, units), BF16),
            pltpu.VMEM((total, units), BF16),
            pltpu.VMEM((2, total // 2, units), BF16),
            pltpu.VMEM((2, total // 2, units), BF16),
            pltpu.VMEM((2, total // 2, units), F32),
            pltpu.VMEM((total, wblk), BF16),
            pltpu.VMEM((2, total, 2 * wblk), BF16),
            pltpu.VMEM((slots, 2 * wblk), BF16),
            pltpu.VMEM((rows, wblk), BF16),
            pltpu.VMEM((rows, wblk), BF16),
            dma((6,)),
            dma((3,)),
            dma((3, GROUPS)),
            dma((3, GROUPS, 2)),
            dma((3, GROUPS, 2)),
            dma((2, GROUPS)),
            dma((2, GROUPS)),
            dma((3, 4)),
            dma((3, 4)),
            dma((3,)),
            dma((3,)),
            dma((3,)),
            dma((4,)),
        ],
        compiler_params=pltpu.CompilerParams(
            collective_id=0, has_side_effects=True, vmem_limit_bytes=63 * 1024 * 1024
        ),
    )(tokens, expert_ids.T, probs.T, refresh_slot, w_in, w_down, fresh_in, fresh_down)


def solution(mesh):
    return jax.shard_map(
        functools.partial(on_device, mesh.shape["wide"]),
        mesh=mesh,
        in_specs=(
            P("wide", None),
            P("wide", None),
            P("wide", None),
            P("wide", None, None, "narrow"),
            P("wide", "narrow", None),
            P(None, "wide", "narrow"),
            P("narrow", "wide"),
            P(),
        ),
        out_specs=P("wide", "narrow"),
        check_vma=False,
    )
```

```python
import functools

import jax
import jax.numpy as jnp
from jax import lax
from jax.experimental import pallas as pl
from jax.experimental.pallas import tpu as pltpu
from jax.sharding import PartitionSpec as P

MESH = pl.DeviceIdType.MESH
CAP = 16
GROUPS = 4
BF16 = jnp.bfloat16
F32 = jnp.float32


def dot(a, b):
    return jnp.dot(a, b, preferred_element_type=F32)


def routing(ids, probs, slots):
    top, rows = ids.shape
    pairs = slots.shape[0]
    experts = 4 * pairs
    q = lax.broadcasted_iota(jnp.int32, (experts, 1), 0)
    kind, pair = q // pairs, q % pairs
    fresh = jnp.zeros((experts, 1), jnp.int32)
    for p in range(pairs):
        fresh = jnp.where(pair == p, slots[p], fresh)
    odd = pair % 2
    kept = 4 * pair + 2 - 2 * odd
    expert = jnp.where(
        kind < 2, kept + kind, jnp.where(kind == 2, 4 * pair + 4 * odd + 1 - fresh, 4 * pair + fresh)
    )
    names = jnp.zeros((experts, rows), F32)
    weight = jnp.zeros((experts, rows), F32)
    for k in range(top):
        hit = ids[k : k + 1] == expert
        names = jnp.where(hit, 1.0, names)
        weight = jnp.where(hit, probs[k : k + 1], weight)
    weight = weight / jnp.sum(probs, axis=0, keepdims=True)
    earlier = lax.broadcasted_iota(jnp.int32, (rows, rows), 0)
    later = lax.broadcasted_iota(jnp.int32, (rows, rows), 1)
    before = jnp.where(earlier < later, 1.0, 0.0).astype(BF16)
    position = dot(names.astype(BF16), before)
    return jnp.where(names > 0.0, position, -1.0).astype(BF16), weight


def spread(kind, pairs):
    row = lax.broadcasted_iota(jnp.int32, (pairs * CAP, 4 * pairs), 0)
    column = lax.broadcasted_iota(jnp.int32, (pairs * CAP, 4 * pairs), 1)
    return jnp.where(row // CAP + kind * pairs == column, 1.0, 0.0).astype(BF16)


def gated(gate, up):
    return (gate / (1.0 + jnp.exp(-gate)) * up).astype(BF16)


def kernel(
    nwide,
    tok_hbm,
    ids_ref,
    probs_ref,
    slot_ref,
    wi_hbm,
    wd_hbm,
    fi_hbm,
    fd_hbm,
    out_ref,
    tok,
    sel,
    coef,
    picked,
    recv_r,
    recv_k,
    wi,
    wd,
    fi,
    fd,
    acc,
    hid,
    hid_r,
    part_out,
    part_in,
    part_own,
    in_r,
    in_k,
    in_x,
    ret,
    mixing,
    mix_out,
    mix_in,
    load_sem,
    dsend,
    drecv,
    fsend,
    frecv,
    csend,
    crecv,
    xsend,
    xrecv,
    osend,
    orecv,
    psend,
    precv,
    rsend,
    rrecv,
):
    rows, wblk = out_ref.shape
    total = nwide * CAP
    half = total // 2
    npair = nwide // 2
    per_kind = npair * CAP
    tile = wblk // 2
    lone = 3 * wblk // 4
    direct = 2 * wblk - lone
    common = wblk - lone
    group = nwide // GROUPS
    span_g = group * CAP
    wide, narrow = lax.axis_index("wide"), lax.axis_index("narrow")
    x_hi = wide // (nwide // 2)
    x_lo, core = narrow // 2, narrow % 2
    pair, side = wide // 2, wide % 2
    pair_odd = pair % 2
    owner = 1 - (side + pair_odd) % 2
    sibling = (wide, x_lo * 2 + 1 - core)
    mate = (wide, (1 - x_lo) * 2 + core)
    partner = (pair * 2 + 1 - side, narrow)

    def peer(index):
        other = (x_lo + x_hi + index // (nwide // 2)) % 2
        return (index, other * 2 + core)

    def turn(i, sign=1):
        plane, step = nwide // 2, i // 2
        if plane == 16:
            z = wide // 4 % 4 + 4 + sign * ((step + step // 4) % 4)
            y = wide % 4 + 4 + sign * (step % 4)
            spot = z % 4 * 4 + y % 4
        else:
            spot = (wide + plane + sign * step) % plane
        return (x_hi + i) % 2 * plane + spot

    def remote(src, dst, send, recv, device):
        return pltpu.make_async_remote_copy(
            src_ref=src, dst_ref=dst, send_sem=send, recv_sem=recv, device_id=device, device_id_type=MESH
        )

    def arrived(ref, sem):
        pltpu.make_async_copy(ref, ref, sem).wait()

    def across(which):
        return pl.ds(pl.multiple_of(which * lone, 128), direct)

    def alone(which):
        return pl.ds(pl.multiple_of(which * direct, 128), lone)

    def block(ref, index):
        return ref.at[pl.ds(pl.multiple_of(index * CAP, CAP), CAP)]

    loads = [
        pltpu.make_async_copy(
            tok_hbm.at[:, pl.ds(pl.multiple_of(core * wblk, wblk), wblk)], tok.at[:, :wblk], load_sem.at[0]
        ),
        pltpu.make_async_copy(
            tok_hbm.at[:, pl.ds(pl.multiple_of((core + 2) * wblk, wblk), wblk)],
            tok.at[:, wblk:],
            load_sem.at[1],
        ),
        pltpu.make_async_copy(fi_hbm, fi, load_sem.at[2]),
        pltpu.make_async_copy(fd_hbm, fd, load_sem.at[3]),
        pltpu.make_async_copy(wi_hbm, wi, load_sem.at[4]),
        pltpu.make_async_copy(wd_hbm, wd, load_sem.at[5]),
    ]
    for load in loads:
        load.start()

    for blank in (pl.ds(0, lone), pl.ds(direct, lone)):
        ret[: 3 * per_kind, blank] = jnp.zeros((3 * per_kind, lone), BF16)

    barrier = pltpu.get_barrier_semaphore()

    def greet(i, carry):
        pl.semaphore_signal(
            barrier, inc=1, device_id=peer(turn(i)), device_id_type=MESH
        )
        return carry

    lax.fori_loop(1, nwide, greet, 0)
    pl.semaphore_signal(barrier, inc=1, device_id=sibling, device_id_type=MESH)
    pl.semaphore_signal(barrier, inc=1, device_id=mate, device_id_type=MESH)

    key, weight = routing(ids_ref[...], probs_ref[...], slot_ref)
    loads[0].wait()
    loads[1].wait()

    def pick(kind):
        span = pl.ds(kind * per_kind, per_kind)
        slot = lax.broadcasted_iota(jnp.int32, (per_kind, rows), 0) % CAP
        chosen = jnp.where(dot(spread(kind, npair), key) == slot.astype(F32), 1.0, 0.0).astype(BF16)
        sel[span, :] = chosen
        picked[span, :] = dot(chosen, tok[...]).astype(BF16)

    pick(0)
    pick(2)
    pl.semaphore_wait(barrier, nwide + 1)

    def incoming(which, chip):
        return across(chip) if which == 0 else pl.ds(0, 2 * wblk)

    def send_kept(i, which, row):
        index = turn(i)
        device = peer(index)
        columns = incoming(which, device[1] // 2)
        remote(
            picked.at[pl.ds(pl.multiple_of(row(index), CAP), CAP), columns],
            block(recv_k.at[which, core], i).at[:, columns],
            dsend.at[which],
            drecv.at[which, i // group],
            device,
        ).start()

    def keep_kept(which, row):
        columns = incoming(which, x_lo)
        pltpu.make_async_copy(
            picked.at[pl.ds(pl.multiple_of(row(wide), CAP), CAP), columns],
            block(recv_k.at[which, core], 0).at[:, columns],
            drecv.at[which, 0],
        ).start()

    def row_0(index):
        to_owner = 1 - (index % 2 + index // 2) % 2
        return to_owner * (2 * per_kind) + index // 2 * CAP

    def send_0(i, carry):
        send_kept(i, 0, row_0)
        return carry

    lax.fori_loop(1, nwide, send_0, 0)
    keep_kept(0, row_0)

    pick(3)

    def piece_r(index):
        return picked.at[
            pl.ds(pl.multiple_of(3 * per_kind + index // 2 * CAP, CAP), CAP),
            pl.ds(pl.multiple_of(index % 2 * wblk, wblk), wblk),
        ]

    def send_r(i, carry):
        index = turn(i)
        remote(
            piece_r(index), block(recv_r.at[core], wide), dsend.at[2], drecv.at[2, 0], peer(index)
        ).start()
        return carry

    lax.fori_loop(1, nwide, send_r, 0)
    pltpu.make_async_copy(piece_r(wide), block(recv_r.at[core], wide), drecv.at[2, 0]).start()

    pick(1)

    def row_1(index):
        return per_kind + index // 2 * CAP

    def send_1(i, carry):
        index = turn(i)

        @pl.when((index % 2 + index // 2) % 2 == 1)
        def _():
            send_kept(i, 1, row_1)

        return carry

    lax.fori_loop(1, nwide, send_1, 0)

    @pl.when(owner == 0)
    def _():
        keep_kept(1, row_1)

    high = weight.astype(BF16)
    low = (weight - high.astype(F32)).astype(BF16)
    for part, value in enumerate((high, low)):
        for kind in range(4):
            span = pl.ds(kind * per_kind, per_kind)
            taken = sel[span, :].astype(F32) * dot(spread(kind, npair), value)
            coef[part * rows : (part + 1) * rows, span] = taken.T.astype(BF16)

    mine = pl.ds(pl.multiple_of(side * half, half), half)
    theirs = pl.ds(pl.multiple_of((1 - side) * half, half), half)
    forward = remote(recv_r.at[core], recv_r.at[core], fsend.at[2, 0, 0], frecv.at[2, 0, 0], sibling)
    swap = remote(part_out, part_in, psend.at[0], precv.at[0], partner)
    share = remote(hid_r.at[mine], hid_r.at[mine], psend.at[1], precv.at[1], partner)

    def fresh_partial():
        arrived(recv_r.at[core], drecv.at[2, 0])
        forward.start()
        loads[2].wait()
        depth = pl.ds(pl.multiple_of(core * wblk, wblk), wblk)
        for g in range(2):
            acc[g] = dot(recv_r[core], fi[g, depth, :])
        forward.wait_recv()
        depth = pl.ds(pl.multiple_of((1 - core) * wblk, wblk), wblk)
        for g in range(2):
            acc[g] += dot(recv_r[1 - core], fi[g, depth, :])
        for g in range(2):
            part_out[g] = acc[g, theirs, :].astype(BF16)
            part_own[g] = acc[g, mine, :]
        swap.start()

    def fresh_hidden():
        swap.wait_recv()
        hid_r[mine, :] = gated(
            part_own[0] + part_in[0].astype(F32), part_own[1] + part_in[1].astype(F32)
        )
        share.start()

    def give(which, t, source, target, span):
        return remote(
            source.at[:, span], target.at[:, span], osend.at[which, t], orecv.at[which, t], sibling
        )

    def fresh_down_and_back():
        loads[3].wait()
        forward.wait_send()
        arrived(hid_r.at[theirs], precv.at[1])
        given = []
        for t in range(2):
            span = pl.ds(t * tile, tile)
            columns = pl.ds(pl.multiple_of((1 - core) * wblk + t * tile, tile), tile)
            recv_r[1 - core, :, span] = dot(hid_r[...], fd[:, columns]).astype(BF16)
            given.append(give(2, t, recv_r.at[1 - core], in_r, span))
            given[t].start()
        for t in range(2):
            span = pl.ds(t * tile, tile)
            columns = pl.ds(pl.multiple_of(core * wblk + t * tile, tile), tile)
            given[t].wait_recv()
            recv_r[core, :, span] = (
                dot(hid_r[...], fd[:, columns]) + in_r[:, span].astype(F32)
            ).astype(BF16)
        slot = ret.at[
            pl.ds(pl.multiple_of(3 * per_kind + pair * CAP, CAP), CAP),
            pl.ds(pl.multiple_of(side * wblk, wblk), wblk),
        ]

        def back(i, carry):
            index = turn(i)
            remote(
                block(recv_r.at[core], index), slot, rsend.at[2], rrecv.at[3], peer(index)
            ).start()
            return carry

        lax.fori_loop(1, nwide, back, 0)
        pltpu.make_async_copy(block(recv_r.at[core], wide), slot, rrecv.at[3]).start()
        for copy in given:
            copy.wait_send()

    unchanged = (slot_ref[pair] + 1) % 2
    far = alone(1 - x_lo)

    def rows_of(which, g, columns, where=core):
        return recv_k.at[which, where, pl.ds(g * span_g, span_g), columns]

    def forward_near(which, g):
        ref = rows_of(which, g, incoming(which, x_lo))
        return remote(ref, ref, fsend.at[which, g, 0], frecv.at[which, g, 0], sibling)

    def forward_far(which, g):
        ref = rows_of(which, g, far)
        return remote(ref, ref, fsend.at[which, g, 1], frecv.at[which, g, 1], sibling)

    def lend(which, g):
        ref = rows_of(which, g, alone(x_lo))
        return remote(ref, ref, csend.at[which, g], crecv.at[which, g], mate)

    def relay(which, g):
        if g < GROUPS:
            arrived(rows_of(which, g, incoming(which, x_lo)), drecv.at[which, g])
            if which == 0:
                lend(which, g).start()
            forward_near(which, g).start()
        if g > 0 and which == 0:
            arrived(rows_of(which, g - 1, far), crecv.at[which, g - 1])
            forward_far(which, g - 1).start()

    def alone_at(where, chip):
        return chip * direct, (where + 2 * chip) * wblk + chip * common

    def common_at(where):
        return (lone, where * wblk + lone), (wblk, (where + 2) * wblk)

    def gate_and_up(which, expert):
        def multiply(where, offset, row, size, first=False):
            offset, row = pl.multiple_of(offset, 128), pl.multiple_of(row, 128)
            for g in range(2):
                part = dot(
                    recv_k[which, where, :, pl.ds(offset, size)], wi[expert, g, pl.ds(row, size), :]
                )
                if first:
                    acc[g] = part
                else:
                    acc[g] += part

        def multiply_alone(where, chip, first=False):
            multiply(where, *alone_at(where, chip), lone, first)

        def multiply_common(where):
            for place in common_at(where):
                multiply(where, *place, common)

        if which == 0:
            multiply_alone(core, x_lo, True)
            multiply_common(core)
            multiply_alone(core, 1 - x_lo)
        else:
            multiply(core, 0, core * wblk, wblk, True)
            multiply(core, wblk, (core + 2) * wblk, wblk)
        for g in range(GROUPS):
            forward_near(which, g).wait_recv()
        if which == 0:
            multiply_alone(1 - core, x_lo)
            multiply_common(1 - core)
            for g in range(GROUPS):
                forward_far(which, g).wait_recv()
            multiply_alone(1 - core, 1 - x_lo)
        else:
            multiply(1 - core, 0, (1 - core) * wblk, wblk)
            multiply(1 - core, wblk, (3 - core) * wblk, wblk)
        hid[...] = gated(acc[0], acc[1])

    def tiles_at(where):
        return (
            (*alone_at(where, 1 - x_lo), lone),
            (*alone_at(where, x_lo), lone),
            *((*place, common) for place in common_at(where)),
        )

    def give_tile(which, t):
        offset, _, size = tiles_at(core)[t]
        span = pl.ds(pl.multiple_of(offset, 128), size)
        return give(which, t, recv_k.at[which, 1 - core], in_k.at[which], span)

    def cross(which):
        return remote(
            recv_k.at[which, core, :, far], in_x.at[which], xsend.at[which], xrecv.at[which], mate
        )

    def send_back(which, kind, columns):
        slot = ret.at[pl.ds(pl.multiple_of(kind * per_kind + pair * CAP, CAP), CAP), columns]

        def back(i, carry):
            remote(
                block(recv_k.at[which, core], i).at[:, columns],
                slot,
                rsend.at[which],
                rrecv.at[kind],
                peer(turn(i, -1)),
            ).start()
            return carry

        lax.fori_loop(1, nwide, back, 0)
        pltpu.make_async_copy(
            block(recv_k.at[which, core], 0).at[:, columns], slot, rrecv.at[kind]
        ).start()

    def down(which, expert, kind):
        for g in range(GROUPS):
            forward_near(which, g).wait_send()
            if which == 0:
                lend(which, g).wait_send()
                forward_far(which, g).wait_send()
        for t, (offset, column, size) in enumerate(tiles_at(1 - core)):
            span = pl.ds(pl.multiple_of(offset, 128), size)
            columns = pl.ds(pl.multiple_of(column, 128), size)
            recv_k[which, 1 - core, :, span] = dot(hid[...], wd[expert, :, columns]).astype(BF16)
            give_tile(which, t).start()

        def own_tile(t):
            offset, column, size = tiles_at(core)[t]
            span = pl.ds(pl.multiple_of(offset, 128), size)
            columns = pl.ds(pl.multiple_of(column, 128), size)
            give_tile(which, t).wait_recv()
            recv_k[which, core, :, span] = (
                dot(hid[...], wd[expert, :, columns]) + in_k[which, :, span].astype(F32)
            ).astype(BF16)

        own_tile(0)
        cross(which).start()
        own_tile(2)
        own_tile(3)
        send_back(which, kind, pl.ds(lone, 2 * common))
        own_tile(1)

    def finish(which, kind):
        cross(which).wait_recv()
        lot = alone(x_lo)
        recv_k[which, core, :, lot] = (
            recv_k[which, core, :, lot].astype(F32) + in_x[which].astype(F32)
        ).astype(BF16)
        send_back(which, kind, lot)
        cross(which).wait_send()
        for t in range(4):
            give_tile(which, t).wait_send()

    first_expert = owner * unchanged
    for g in range(GROUPS + 1):
        relay(0, g)
    loads[4].wait()
    loads[5].wait()
    gate_and_up(0, first_expert)
    down(0, first_expert, owner * 2)
    fresh_partial()

    @pl.when(owner == 0)
    def _():
        relay(1, 0)
        relay(1, 1)

    finish(0, owner * 2)

    @pl.when(owner == 0)
    def _():
        for g in range(2, GROUPS):
            relay(1, g)
        gate_and_up(1, 1)
        down(1, 1, 1)

    fresh_hidden()
    fresh_down_and_back()

    @pl.when(owner == 0)
    def _():
        finish(1, 1)

    for kind in (0, 2, 3, 1):
        span = pl.ds(kind * per_kind, per_kind)
        if kind == 3:
            arrived(ret.at[span], rrecv.at[kind])
        else:
            arrived(ret.at[span, across(x_lo)], rrecv.at[kind])
        for chip in range(2):
            columns = pl.ds(pl.multiple_of((x_lo + 1 - chip) % 2 * wblk, wblk), wblk)
            both = dot(coef[:, span], ret[span, columns])
            if kind == 0:
                mixing[chip] = both[:rows] + both[rows:]
            else:
                mixing[chip] += both[:rows] + both[rows:]
    mix_out[...] = mixing[0].astype(BF16)
    last = remote(mix_out, mix_in, psend.at[2], precv.at[2], mate)
    last.start()
    last.wait_recv()
    out_ref[...] = (mixing[1] + mix_in[...].astype(F32)).astype(BF16)

    swap.wait_send()
    share.wait_send()
    last.wait_send()
    sent = total - CAP
    arrived(recv_r.at[0, pl.ds(0, sent)], dsend.at[2])
    arrived(recv_r.at[0, pl.ds(0, sent)], rsend.at[2])
    arrived(recv_k.at[0, 0, pl.ds(0, sent), :direct], dsend.at[0])
    arrived(recv_k.at[0, 0, pl.ds(0, sent), :direct], rsend.at[0])

    @pl.when(owner == 1)
    def _():
        arrived(recv_k.at[0, 0, pl.ds(0, per_kind)], dsend.at[1])

    @pl.when(owner == 0)
    def _():
        arrived(recv_k.at[0, 0, pl.ds(0, per_kind - CAP)], dsend.at[1])
        arrived(recv_k.at[0, 0, pl.ds(0, sent), :direct], rsend.at[1])


def on_device(nwide, tokens, expert_ids, probs, w_in, w_down, fresh_in, fresh_down, refresh_slot):
    rows, width = tokens.shape
    units = w_down.shape[1]
    wblk = width // 4
    total = nwide * CAP
    slots = 2 * total
    dma = pltpu.SemaphoreType.DMA
    hbm = pl.BlockSpec(memory_space=pl.ANY)
    vmem = pl.BlockSpec(memory_space=pltpu.VMEM)
    return pl.pallas_call(
        functools.partial(kernel, nwide),
        out_shape=jax.ShapeDtypeStruct((rows, wblk), BF16),
        in_specs=[hbm, vmem, vmem, pl.BlockSpec(memory_space=pltpu.SMEM), hbm, hbm, hbm, hbm],
        out_specs=vmem,
        scratch_shapes=[
            pltpu.VMEM((rows, 2 * wblk), BF16),
            pltpu.VMEM((slots, rows), BF16),
            pltpu.VMEM((2 * rows, slots), BF16),
            pltpu.VMEM((slots, 2 * wblk), BF16),
            pltpu.VMEM((2, total, wblk), BF16),
            pltpu.VMEM((2, 2, total, 2 * wblk), BF16),
            pltpu.VMEM(w_in.shape, BF16),
            pltpu.VMEM(w_down.shape, BF16),
            pltpu.VMEM(fresh_in.shape, BF16),
            pltpu.VMEM(fresh_down.shape, BF16),
            pltpu.VMEM((2, total, units), F32),
            pltpu.VMEM((total, units), BF16),
            pltpu.VMEM((total, units), BF16),
            pltpu.VMEM((2, total // 2, units), BF16),
            pltpu.VMEM((2, total // 2, units), BF16),
            pltpu.VMEM((2, total // 2, units), F32),
            pltpu.VMEM((total, wblk), BF16),
            pltpu.VMEM((2, total, 2 * wblk), BF16),
            pltpu.VMEM((2, total, wblk * 3 // 4), BF16),
            pltpu.VMEM((slots, 2 * wblk), BF16),
            pltpu.VMEM((2, rows, wblk), F32),
            pltpu.VMEM((rows, wblk), BF16),
            pltpu.VMEM((rows, wblk), BF16),
            dma((6,)),
            dma((3,)),
            dma((3, GROUPS)),
            dma((3, GROUPS, 2)),
            dma((3, GROUPS, 2)),
            dma((2, GROUPS)),
            dma((2, GROUPS)),
            dma((2,)),
            dma((2,)),
            dma((3, 4)),
            dma((3, 4)),
            dma((3,)),
            dma((3,)),
            dma((3,)),
            dma((4,)),
        ],
        compiler_params=pltpu.CompilerParams(
            collective_id=0, has_side_effects=True, vmem_limit_bytes=63 * 1024 * 1024
        ),
    )(tokens, expert_ids.T, probs.T, refresh_slot, w_in, w_down, fresh_in, fresh_down)


def solution(mesh):
    return jax.shard_map(
        functools.partial(on_device, mesh.shape["wide"]),
        mesh=mesh,
        in_specs=(
            P("wide", None),
            P("wide", None),
            P("wide", None),
            P("wide", None, None, "narrow"),
            P("wide", "narrow", None),
            P(None, "wide", "narrow"),
            P("narrow", "wide"),
            P(),
        ),
        out_specs=P("wide", "narrow"),
        check_vma=False,
    )
```

```python
import functools

import jax
import jax.numpy as jnp
from jax import lax
from jax.experimental import pallas as pl
from jax.experimental.pallas import tpu as pltpu
from jax.sharding import PartitionSpec as P

MESH = pl.DeviceIdType.MESH
CAP = 16
GROUPS = 4
HALVES = 2
BF16 = jnp.bfloat16
F32 = jnp.float32


def dot(a, b):
    return jnp.dot(a, b, preferred_element_type=F32)


def routing(ids, probs, slots):
    top, rows = ids.shape
    pairs = slots.shape[0]
    experts = 4 * pairs
    q = lax.broadcasted_iota(jnp.int32, (experts, 1), 0)
    kind, pair = q // pairs, q % pairs
    fresh = jnp.zeros((experts, 1), jnp.int32)
    for p in range(pairs):
        fresh = jnp.where(pair == p, slots[p], fresh)
    odd = pair % 2
    kept = 4 * pair + 2 - 2 * odd
    expert = jnp.where(
        kind < 2, kept + kind, jnp.where(kind == 2, 4 * pair + 4 * odd + 1 - fresh, 4 * pair + fresh)
    )
    names = jnp.zeros((experts, rows), F32)
    weight = jnp.zeros((experts, rows), F32)
    for k in range(top):
        hit = ids[k : k + 1] == expert
        names = jnp.where(hit, 1.0, names)
        weight = jnp.where(hit, probs[k : k + 1], weight)
    weight = weight / jnp.sum(probs, axis=0, keepdims=True)
    earlier = lax.broadcasted_iota(jnp.int32, (rows, rows), 0)
    later = lax.broadcasted_iota(jnp.int32, (rows, rows), 1)
    before = jnp.where(earlier < later, 1.0, 0.0).astype(BF16)
    position = dot(names.astype(BF16), before)
    return jnp.where(names > 0.0, position, -1.0).astype(BF16), weight


def spread(kind, pairs):
    row = lax.broadcasted_iota(jnp.int32, (pairs * CAP, 4 * pairs), 0)
    column = lax.broadcasted_iota(jnp.int32, (pairs * CAP, 4 * pairs), 1)
    return jnp.where(row // CAP + kind * pairs == column, 1.0, 0.0).astype(BF16)


def gated(gate, up):
    return (gate / (1.0 + jnp.exp(-gate)) * up).astype(BF16)


def kernel(
    nwide,
    tok_hbm,
    ids_ref,
    probs_ref,
    slot_ref,
    wi_hbm,
    wd_hbm,
    fi_hbm,
    fd_hbm,
    out_ref,
    tok,
    sel,
    coef,
    picked,
    recv_r,
    recv_k,
    wi,
    wd,
    fi,
    fd,
    acc,
    hid,
    hid_r,
    part_out,
    part_in,
    part_own,
    in_r,
    in_k,
    in_x,
    ret,
    mixing,
    mix_out,
    mix_in,
    load_sem,
    dsend,
    drecv,
    fsend,
    frecv,
    csend,
    crecv,
    xsend,
    xrecv,
    osend,
    orecv,
    psend,
    precv,
    rsend,
    rrecv,
):
    rows, wblk = out_ref.shape
    total = nwide * CAP
    half = total // 2
    npair = nwide // 2
    per_kind = npair * CAP
    tile = wblk // 2
    lone = 7 * wblk // 8
    direct = 2 * wblk - lone
    common = wblk - lone
    group = nwide // GROUPS
    span_g = group * CAP
    wide, narrow = lax.axis_index("wide"), lax.axis_index("narrow")
    x_hi = wide // (nwide // 2)
    x_lo, core = narrow // 2, narrow % 2
    pair, side = wide // 2, wide % 2
    pair_odd = pair % 2
    owner = 1 - (side + pair_odd) % 2
    sibling = (wide, x_lo * 2 + 1 - core)
    mate = (wide, (1 - x_lo) * 2 + core)
    partner = (pair * 2 + 1 - side, narrow)

    def peer(index):
        other = (x_lo + x_hi + index // (nwide // 2)) % 2
        return (index, other * 2 + core)

    def turn(i, sign=1):
        plane, step = nwide // 2, i // 2
        if plane == 16:
            z = wide // 4 % 4 + 4 + sign * ((step + step // 4) % 4)
            y = wide % 4 + 4 + sign * (step % 4)
            spot = z % 4 * 4 + y % 4
        else:
            spot = (wide + plane + sign * step) % plane
        return (x_hi + i) % 2 * plane + spot

    def remote(src, dst, send, recv, device):
        return pltpu.make_async_remote_copy(
            src_ref=src, dst_ref=dst, send_sem=send, recv_sem=recv, device_id=device, device_id_type=MESH
        )

    def arrived(ref, sem):
        pltpu.make_async_copy(ref, ref, sem).wait()

    def across(which):
        return pl.ds(pl.multiple_of(which * lone, 128), direct)

    def alone(which):
        return pl.ds(pl.multiple_of(which * direct, 128), lone)

    def block(ref, index):
        return ref.at[pl.ds(pl.multiple_of(index * CAP, CAP), CAP)]

    loads = [
        pltpu.make_async_copy(
            tok_hbm.at[:, pl.ds(pl.multiple_of(core * wblk, wblk), wblk)], tok.at[:, :wblk], load_sem.at[0]
        ),
        pltpu.make_async_copy(
            tok_hbm.at[:, pl.ds(pl.multiple_of((core + 2) * wblk, wblk), wblk)],
            tok.at[:, wblk:],
            load_sem.at[1],
        ),
        pltpu.make_async_copy(fi_hbm, fi, load_sem.at[2]),
        pltpu.make_async_copy(fd_hbm, fd, load_sem.at[3]),
        pltpu.make_async_copy(wi_hbm, wi, load_sem.at[4]),
        pltpu.make_async_copy(wd_hbm, wd, load_sem.at[5]),
    ]
    for load in loads:
        load.start()

    for blank in (pl.ds(0, lone), pl.ds(direct, lone)):
        ret[: 3 * per_kind, blank] = jnp.zeros((3 * per_kind, lone), BF16)

    barrier = pltpu.get_barrier_semaphore()

    def greet(i, carry):
        pl.semaphore_signal(
            barrier, inc=1, device_id=peer(turn(i)), device_id_type=MESH
        )
        return carry

    lax.fori_loop(1, nwide, greet, 0)
    pl.semaphore_signal(barrier, inc=1, device_id=sibling, device_id_type=MESH)
    pl.semaphore_signal(barrier, inc=1, device_id=mate, device_id_type=MESH)

    key, weight = routing(ids_ref[...], probs_ref[...], slot_ref)
    loads[0].wait()
    loads[1].wait()

    def pick(kind):
        span = pl.ds(kind * per_kind, per_kind)
        slot = lax.broadcasted_iota(jnp.int32, (per_kind, rows), 0) % CAP
        chosen = jnp.where(dot(spread(kind, npair), key) == slot.astype(F32), 1.0, 0.0).astype(BF16)
        sel[span, :] = chosen
        picked[span, :] = dot(chosen, tok[...]).astype(BF16)

    pick(0)
    pick(2)
    pl.semaphore_wait(barrier, nwide + 1)

    def incoming(which, chip):
        return across(chip) if which == 0 else pl.ds(0, 2 * wblk)

    def send_kept(i, which, row):
        index = turn(i)
        device = peer(index)
        columns = incoming(which, device[1] // 2)
        remote(
            picked.at[pl.ds(pl.multiple_of(row(index), CAP), CAP), columns],
            block(recv_k.at[which, core], i).at[:, columns],
            dsend.at[which],
            drecv.at[which, i // group],
            device,
        ).start()

    def keep_kept(which, row):
        columns = incoming(which, x_lo)
        pltpu.make_async_copy(
            picked.at[pl.ds(pl.multiple_of(row(wide), CAP), CAP), columns],
            block(recv_k.at[which, core], 0).at[:, columns],
            drecv.at[which, 0],
        ).start()

    def row_0(index):
        to_owner = 1 - (index % 2 + index // 2) % 2
        return to_owner * (2 * per_kind) + index // 2 * CAP

    def send_0(i, carry):
        send_kept(i, 0, row_0)
        return carry

    lax.fori_loop(1, nwide, send_0, 0)
    keep_kept(0, row_0)

    pick(3)

    def piece_r(index):
        return picked.at[
            pl.ds(pl.multiple_of(3 * per_kind + index // 2 * CAP, CAP), CAP),
            pl.ds(pl.multiple_of(index % 2 * wblk, wblk), wblk),
        ]

    def send_r(i, carry):
        index = turn(i)
        remote(
            piece_r(index), block(recv_r.at[core], wide), dsend.at[2], drecv.at[2, 0], peer(index)
        ).start()
        return carry

    lax.fori_loop(1, nwide, send_r, 0)
    pltpu.make_async_copy(piece_r(wide), block(recv_r.at[core], wide), drecv.at[2, 0]).start()

    pick(1)

    def row_1(index):
        return per_kind + index // 2 * CAP

    def send_1(i, carry):
        index = turn(i)

        @pl.when((index % 2 + index // 2) % 2 == 1)
        def _():
            send_kept(i, 1, row_1)

        return carry

    lax.fori_loop(1, nwide, send_1, 0)

    @pl.when(owner == 0)
    def _():
        keep_kept(1, row_1)

    high = weight.astype(BF16)
    low = (weight - high.astype(F32)).astype(BF16)
    for part, value in enumerate((high, low)):
        for kind in range(4):
            span = pl.ds(kind * per_kind, per_kind)
            taken = sel[span, :].astype(F32) * dot(spread(kind, npair), value)
            coef[part * rows : (part + 1) * rows, span] = taken.T.astype(BF16)

    mine = pl.ds(pl.multiple_of(side * half, half), half)
    theirs = pl.ds(pl.multiple_of((1 - side) * half, half), half)
    forward = remote(recv_r.at[core], recv_r.at[core], fsend.at[2, 0, 0], frecv.at[2, 0, 0], sibling)
    swap = remote(part_out, part_in, psend.at[0], precv.at[0], partner)
    share = remote(hid_r.at[mine], hid_r.at[mine], psend.at[1], precv.at[1], partner)

    def fresh_partial():
        arrived(recv_r.at[core], drecv.at[2, 0])
        forward.start()
        loads[2].wait()
        depth = pl.ds(pl.multiple_of(core * wblk, wblk), wblk)
        for g in range(2):
            acc[g] = dot(recv_r[core], fi[g, depth, :])
        forward.wait_recv()
        depth = pl.ds(pl.multiple_of((1 - core) * wblk, wblk), wblk)
        for g in range(2):
            acc[g] += dot(recv_r[1 - core], fi[g, depth, :])
        for g in range(2):
            part_out[g] = acc[g, theirs, :].astype(BF16)
            part_own[g] = acc[g, mine, :]
        swap.start()

    def fresh_hidden():
        swap.wait_recv()
        hid_r[mine, :] = gated(
            part_own[0] + part_in[0].astype(F32), part_own[1] + part_in[1].astype(F32)
        )
        share.start()

    def give(which, part, t, source, target, span):
        return remote(
            source.at[:, span],
            target.at[:, span],
            osend.at[which, part, t],
            orecv.at[which, part, t],
            sibling,
        )

    def fresh_down_and_back():
        loads[3].wait()
        forward.wait_send()
        arrived(hid_r.at[theirs], precv.at[1])
        given = []
        for t in range(2):
            span = pl.ds(t * tile, tile)
            columns = pl.ds(pl.multiple_of((1 - core) * wblk + t * tile, tile), tile)
            recv_r[1 - core, :, span] = dot(hid_r[...], fd[:, columns]).astype(BF16)
            given.append(give(2, 0, t, recv_r.at[1 - core], in_r, span))
            given[t].start()
        for t in range(2):
            span = pl.ds(t * tile, tile)
            columns = pl.ds(pl.multiple_of(core * wblk + t * tile, tile), tile)
            given[t].wait_recv()
            recv_r[core, :, span] = (
                dot(hid_r[...], fd[:, columns]) + in_r[:, span].astype(F32)
            ).astype(BF16)
        slot = ret.at[
            pl.ds(pl.multiple_of(3 * per_kind + pair * CAP, CAP), CAP),
            pl.ds(pl.multiple_of(side * wblk, wblk), wblk),
        ]

        def back(i, carry):
            index = turn(i)
            remote(
                block(recv_r.at[core], index), slot, rsend.at[2], rrecv.at[3], peer(index)
            ).start()
            return carry

        lax.fori_loop(1, nwide, back, 0)
        pltpu.make_async_copy(block(recv_r.at[core], wide), slot, rrecv.at[3]).start()
        for copy in given:
            copy.wait_send()

    unchanged = (slot_ref[pair] + 1) % 2
    far = alone(1 - x_lo)

    def rows_of(which, g, columns, where=core):
        return recv_k.at[which, where, pl.ds(g * span_g, span_g), columns]

    def forward_near(which, g):
        ref = rows_of(which, g, incoming(which, x_lo))
        return remote(ref, ref, fsend.at[which, g, 0], frecv.at[which, g, 0], sibling)

    def forward_far(which, g):
        ref = rows_of(which, g, far)
        return remote(ref, ref, fsend.at[which, g, 1], frecv.at[which, g, 1], sibling)

    def lend(which, g):
        ref = rows_of(which, g, alone(x_lo))
        return remote(ref, ref, csend.at[which, g], crecv.at[which, g], mate)

    def relay(which, g):
        arrived(rows_of(which, g, incoming(which, x_lo)), drecv.at[which, g])
        if which == 0:
            lend(which, g).start()
        forward_near(which, g).start()

    def relay_far(which, g):
        arrived(rows_of(which, g, far), crecv.at[which, g])
        forward_far(which, g).start()

    def alone_at(where, chip):
        return chip * direct, (where + 2 * chip) * wblk + chip * common

    def common_at(where):
        return (lone, where * wblk + lone), (wblk, (where + 2) * wblk)

    def half_of(part):
        return pl.ds(part * half, half)

    def groups_of(part):
        return range(part * GROUPS // HALVES, (part + 1) * GROUPS // HALVES)

    def gate_and_up(which, part, expert):
        here = half_of(part)

        def multiply(where, offset, row, size, first=False):
            offset, row = pl.multiple_of(offset, 128), pl.multiple_of(row, 128)
            for g in range(2):
                term = dot(
                    recv_k[which, where, here, pl.ds(offset, size)],
                    wi[expert, g, pl.ds(row, size), :],
                )
                if first:
                    acc[g, here, :] = term
                else:
                    acc[g, here, :] += term

        def multiply_alone(where, chip, first=False):
            multiply(where, *alone_at(where, chip), lone, first)

        def multiply_common(where):
            for place in common_at(where):
                multiply(where, *place, common)

        if which == 0:
            multiply_alone(core, x_lo, True)
            multiply_common(core)
            multiply_alone(core, 1 - x_lo)
        else:
            multiply(core, 0, core * wblk, wblk, True)
            multiply(core, wblk, (core + 2) * wblk, wblk)
        for g in groups_of(part):
            forward_near(which, g).wait_recv()
        if which == 0:
            multiply_alone(1 - core, x_lo)
            multiply_common(1 - core)
            for g in groups_of(part):
                forward_far(which, g).wait_recv()
            multiply_alone(1 - core, 1 - x_lo)
        else:
            multiply(1 - core, 0, (1 - core) * wblk, wblk)
            multiply(1 - core, wblk, (3 - core) * wblk, wblk)
        hid[here, :] = gated(acc[0, here, :], acc[1, here, :])

    def tiles_at(where):
        return (
            (*alone_at(where, 1 - x_lo), lone),
            (*alone_at(where, x_lo), lone),
            *((*place, common) for place in common_at(where)),
        )

    def give_tile(which, part, t):
        offset, _, size = tiles_at(core)[t]
        here = half_of(part)
        return give(
            which,
            part,
            t,
            recv_k.at[which, 1 - core, here],
            in_k.at[which, here],
            pl.ds(pl.multiple_of(offset, 128), size),
        )

    def cross(which, part):
        here = half_of(part)
        return remote(
            recv_k.at[which, core, here, far],
            in_x.at[which, here],
            xsend.at[which, part],
            xrecv.at[which, part],
            mate,
        )

    def send_back(which, part, kind, columns):
        slot = ret.at[pl.ds(pl.multiple_of(kind * per_kind + pair * CAP, CAP), CAP), columns]

        def back(i, carry):
            remote(
                block(recv_k.at[which, core], i).at[:, columns],
                slot,
                rsend.at[which],
                rrecv.at[kind],
                peer(turn(i, -1)),
            ).start()
            return carry

        each = nwide // HALVES
        lax.fori_loop(max(1, part * each), (part + 1) * each, back, 0)
        if part == 0:
            pltpu.make_async_copy(
                block(recv_k.at[which, core], 0).at[:, columns], slot, rrecv.at[kind]
            ).start()

    def down(which, part, expert, kind):
        here = half_of(part)
        for g in groups_of(part):
            forward_near(which, g).wait_send()
            if which == 0:
                lend(which, g).wait_send()
                forward_far(which, g).wait_send()
        for t, (offset, column, size) in enumerate(tiles_at(1 - core)):
            span = pl.ds(pl.multiple_of(offset, 128), size)
            columns = pl.ds(pl.multiple_of(column, 128), size)
            recv_k[which, 1 - core, here, span] = dot(
                hid[here, :], wd[expert, :, columns]
            ).astype(BF16)
            give_tile(which, part, t).start()

        def own_tile(t):
            offset, column, size = tiles_at(core)[t]
            span = pl.ds(pl.multiple_of(offset, 128), size)
            columns = pl.ds(pl.multiple_of(column, 128), size)
            give_tile(which, part, t).wait_recv()
            recv_k[which, core, here, span] = (
                dot(hid[here, :], wd[expert, :, columns]) + in_k[which, here, span].astype(F32)
            ).astype(BF16)

        own_tile(0)
        cross(which, part).start()
        own_tile(2)
        own_tile(3)
        send_back(which, part, kind, pl.ds(lone, 2 * common))
        own_tile(1)

    def finish(which, part, kind):
        here = half_of(part)
        cross(which, part).wait_recv()
        lot = alone(x_lo)
        recv_k[which, core, here, lot] = (
            recv_k[which, core, here, lot].astype(F32) + in_x[which, here].astype(F32)
        ).astype(BF16)
        send_back(which, part, kind, lot)

    def settle(which):
        for part in range(HALVES):
            cross(which, part).wait_send()
            for t in range(4):
                give_tile(which, part, t).wait_send()

    first_expert = owner * unchanged
    first_kind = owner * 2
    for g in range(GROUPS):
        relay(0, g)
        if g > 0:
            relay_far(0, g - 1)
    loads[4].wait()
    loads[5].wait()
    gate_and_up(0, 0, first_expert)
    relay_far(0, GROUPS - 1)
    down(0, 0, first_expert, first_kind)
    gate_and_up(0, 1, first_expert)
    down(0, 1, first_expert, first_kind)
    fresh_partial()
    finish(0, 0, first_kind)

    @pl.when(owner == 0)
    def _():
        relay(1, 0)
        relay(1, 1)

    finish(0, 1, first_kind)

    @pl.when(owner == 0)
    def _():
        gate_and_up(1, 0, 1)
        down(1, 0, 1, 1)
        for g in range(2, GROUPS):
            relay(1, g)
        gate_and_up(1, 1, 1)
        down(1, 1, 1, 1)

    fresh_hidden()

    @pl.when(owner == 0)
    def _():
        finish(1, 0, 1)

    fresh_down_and_back()

    @pl.when(owner == 0)
    def _():
        finish(1, 1, 1)
        settle(1)

    settle(0)

    for kind in (0, 2, 3, 1):
        span = pl.ds(kind * per_kind, per_kind)
        if kind == 3:
            arrived(ret.at[span], rrecv.at[kind])
        else:
            arrived(ret.at[span, across(x_lo)], rrecv.at[kind])
        for chip in range(2):
            columns = pl.ds(pl.multiple_of((x_lo + 1 - chip) % 2 * wblk, wblk), wblk)
            both = dot(coef[:, span], ret[span, columns])
            if kind == 0:
                mixing[chip] = both[:rows] + both[rows:]
            else:
                mixing[chip] += both[:rows] + both[rows:]
    mix_out[...] = mixing[0].astype(BF16)
    last = remote(mix_out, mix_in, psend.at[2], precv.at[2], mate)
    last.start()
    last.wait_recv()
    out_ref[...] = (mixing[1] + mix_in[...].astype(F32)).astype(BF16)

    swap.wait_send()
    share.wait_send()
    last.wait_send()
    sent = total - CAP
    arrived(recv_r.at[0, pl.ds(0, sent)], dsend.at[2])
    arrived(recv_r.at[0, pl.ds(0, sent)], rsend.at[2])
    arrived(recv_k.at[0, 0, pl.ds(0, sent), :direct], dsend.at[0])
    arrived(recv_k.at[0, 0, pl.ds(0, sent), :direct], rsend.at[0])

    @pl.when(owner == 1)
    def _():
        arrived(recv_k.at[0, 0, pl.ds(0, per_kind)], dsend.at[1])

    @pl.when(owner == 0)
    def _():
        arrived(recv_k.at[0, 0, pl.ds(0, per_kind - CAP)], dsend.at[1])
        arrived(recv_k.at[0, 0, pl.ds(0, sent), :direct], rsend.at[1])


def on_device(nwide, tokens, expert_ids, probs, w_in, w_down, fresh_in, fresh_down, refresh_slot):
    rows, width = tokens.shape
    units = w_down.shape[1]
    wblk = width // 4
    total = nwide * CAP
    slots = 2 * total
    dma = pltpu.SemaphoreType.DMA
    hbm = pl.BlockSpec(memory_space=pl.ANY)
    vmem = pl.BlockSpec(memory_space=pltpu.VMEM)
    return pl.pallas_call(
        functools.partial(kernel, nwide),
        out_shape=jax.ShapeDtypeStruct((rows, wblk), BF16),
        in_specs=[hbm, vmem, vmem, pl.BlockSpec(memory_space=pltpu.SMEM), hbm, hbm, hbm, hbm],
        out_specs=vmem,
        scratch_shapes=[
            pltpu.VMEM((rows, 2 * wblk), BF16),
            pltpu.VMEM((slots, rows), BF16),
            pltpu.VMEM((2 * rows, slots), BF16),
            pltpu.VMEM((slots, 2 * wblk), BF16),
            pltpu.VMEM((2, total, wblk), BF16),
            pltpu.VMEM((2, 2, total, 2 * wblk), BF16),
            pltpu.VMEM(w_in.shape, BF16),
            pltpu.VMEM(w_down.shape, BF16),
            pltpu.VMEM(fresh_in.shape, BF16),
            pltpu.VMEM(fresh_down.shape, BF16),
            pltpu.VMEM((2, total, units), F32),
            pltpu.VMEM((total, units), BF16),
            pltpu.VMEM((total, units), BF16),
            pltpu.VMEM((2, total // 2, units), BF16),
            pltpu.VMEM((2, total // 2, units), BF16),
            pltpu.VMEM((2, total // 2, units), F32),
            pltpu.VMEM((total, wblk), BF16),
            pltpu.VMEM((2, total, 2 * wblk), BF16),
            pltpu.VMEM((2, total, wblk * 7 // 8), BF16),
            pltpu.VMEM((slots, 2 * wblk), BF16),
            pltpu.VMEM((2, rows, wblk), F32),
            pltpu.VMEM((rows, wblk), BF16),
            pltpu.VMEM((rows, wblk), BF16),
            dma((6,)),
            dma((3,)),
            dma((3, GROUPS)),
            dma((3, GROUPS, 2)),
            dma((3, GROUPS, 2)),
            dma((2, GROUPS)),
            dma((2, GROUPS)),
            dma((2, HALVES)),
            dma((2, HALVES)),
            dma((3, HALVES, 4)),
            dma((3, HALVES, 4)),
            dma((3,)),
            dma((3,)),
            dma((3,)),
            dma((4,)),
        ],
        compiler_params=pltpu.CompilerParams(
            collective_id=0, has_side_effects=True, vmem_limit_bytes=63 * 1024 * 1024
        ),
    )(tokens, expert_ids.T, probs.T, refresh_slot, w_in, w_down, fresh_in, fresh_down)


def solution(mesh):
    return jax.shard_map(
        functools.partial(on_device, mesh.shape["wide"]),
        mesh=mesh,
        in_specs=(
            P("wide", None),
            P("wide", None),
            P("wide", None),
            P("wide", None, None, "narrow"),
            P("wide", "narrow", None),
            P(None, "wide", "narrow"),
            P("narrow", "wide"),
            P(),
        ),
        out_specs=P("wide", "narrow"),
        check_vma=False,
    )
```

```python
import functools

import jax
import jax.numpy as jnp
from jax import lax
from jax.experimental import pallas as pl
from jax.experimental.pallas import tpu as pltpu
from jax.sharding import PartitionSpec as P

MESH = pl.DeviceIdType.MESH
CAP = 16
GROUPS = 4
HALVES = 2
BF16 = jnp.bfloat16
F32 = jnp.float32


def dot(a, b):
    return jnp.dot(a, b, preferred_element_type=F32)


def routing(ids, probs, slots):
    top, rows = ids.shape
    pairs = slots.shape[0]
    experts = 4 * pairs
    q = lax.broadcasted_iota(jnp.int32, (experts, 1), 0)
    kind, pair = q // pairs, q % pairs
    fresh = jnp.zeros((experts, 1), jnp.int32)
    for p in range(pairs):
        fresh = jnp.where(pair == p, slots[p], fresh)
    odd = pair % 2
    kept = 4 * pair + 2 - 2 * odd
    expert = jnp.where(
        kind < 2, kept + kind, jnp.where(kind == 2, 4 * pair + 4 * odd + 1 - fresh, 4 * pair + fresh)
    )
    names = jnp.zeros((experts, rows), F32)
    weight = jnp.zeros((experts, rows), F32)
    for k in range(top):
        hit = ids[k : k + 1] == expert
        names = jnp.where(hit, 1.0, names)
        weight = jnp.where(hit, probs[k : k + 1], weight)
    weight = weight / jnp.sum(probs, axis=0, keepdims=True)
    earlier = lax.broadcasted_iota(jnp.int32, (rows, rows), 0)
    later = lax.broadcasted_iota(jnp.int32, (rows, rows), 1)
    before = jnp.where(earlier < later, 1.0, 0.0).astype(BF16)
    position = dot(names.astype(BF16), before)
    return jnp.where(names > 0.0, position, -1.0).astype(BF16), weight


def spread(kind, pairs):
    row = lax.broadcasted_iota(jnp.int32, (pairs * CAP, 4 * pairs), 0)
    column = lax.broadcasted_iota(jnp.int32, (pairs * CAP, 4 * pairs), 1)
    return jnp.where(row // CAP + kind * pairs == column, 1.0, 0.0).astype(BF16)


def gated(gate, up):
    return (gate / (1.0 + jnp.exp(-gate)) * up).astype(BF16)


def kernel(
    nwide,
    tok_hbm,
    ids_ref,
    probs_ref,
    slot_ref,
    wi_hbm,
    wd_hbm,
    fi_hbm,
    fd_hbm,
    out_ref,
    tok,
    sel,
    coef,
    picked,
    recv_r,
    recv_k,
    wi,
    wd,
    fi,
    fd,
    acc,
    hid,
    hid_r,
    part_out,
    part_in,
    part_own,
    in_r,
    in_k,
    in_x,
    ret,
    mixing,
    mix_out,
    mix_in,
    load_sem,
    dsend,
    drecv,
    fsend,
    frecv,
    csend,
    crecv,
    xsend,
    xrecv,
    osend,
    orecv,
    psend,
    precv,
    rsend,
    rrecv,
):
    rows, wblk = out_ref.shape
    total = nwide * CAP
    half = total // 2
    npair = nwide // 2
    per_kind = npair * CAP
    tile = wblk // 2
    lone = 7 * wblk // 8
    direct = 2 * wblk - lone
    common = wblk - lone
    group = nwide // GROUPS
    span_g = group * CAP
    wide, narrow = lax.axis_index("wide"), lax.axis_index("narrow")
    x_hi = wide // (nwide // 2)
    x_lo, core = narrow // 2, narrow % 2
    pair, side = wide // 2, wide % 2
    pair_odd = pair % 2
    owner = 1 - (side + pair_odd) % 2
    sibling = (wide, x_lo * 2 + 1 - core)
    mate = (wide, (1 - x_lo) * 2 + core)
    partner = (pair * 2 + 1 - side, narrow)

    def peer(index):
        other = (x_lo + x_hi + index // (nwide // 2)) % 2
        return (index, other * 2 + core)

    def turn(i, sign=1):
        plane, step = nwide // 2, i // 2
        if plane == 16:
            z = wide // 4 % 4 + 4 + sign * ((step + step // 4) % 4)
            y = wide % 4 + 4 + sign * (step % 4)
            spot = z % 4 * 4 + y % 4
        else:
            spot = (wide + plane + sign * step) % plane
        return (x_hi + i) % 2 * plane + spot

    def remote(src, dst, send, recv, device):
        return pltpu.make_async_remote_copy(
            src_ref=src, dst_ref=dst, send_sem=send, recv_sem=recv, device_id=device, device_id_type=MESH
        )

    def arrived(ref, sem):
        pltpu.make_async_copy(ref, ref, sem).wait()

    def across(which):
        return pl.ds(pl.multiple_of(which * lone, 128), direct)

    def alone(which):
        return pl.ds(pl.multiple_of(which * direct, 128), lone)

    def block(ref, index):
        return ref.at[pl.ds(pl.multiple_of(index * CAP, CAP), CAP)]

    loads = [
        pltpu.make_async_copy(
            tok_hbm.at[:, pl.ds(pl.multiple_of(core * wblk, wblk), wblk)], tok.at[:, :wblk], load_sem.at[0]
        ),
        pltpu.make_async_copy(
            tok_hbm.at[:, pl.ds(pl.multiple_of((core + 2) * wblk, wblk), wblk)],
            tok.at[:, wblk:],
            load_sem.at[1],
        ),
        pltpu.make_async_copy(fi_hbm, fi, load_sem.at[2]),
        pltpu.make_async_copy(fd_hbm, fd, load_sem.at[3]),
        pltpu.make_async_copy(wi_hbm, wi, load_sem.at[4]),
        pltpu.make_async_copy(wd_hbm, wd, load_sem.at[5]),
    ]
    for load in loads:
        load.start()

    for blank in (pl.ds(0, lone), pl.ds(direct, lone)):
        ret[: 3 * per_kind, blank] = jnp.zeros((3 * per_kind, lone), BF16)

    barrier = pltpu.get_barrier_semaphore()

    def greet(i, carry):
        pl.semaphore_signal(
            barrier, inc=1, device_id=peer(turn(i)), device_id_type=MESH
        )
        return carry

    lax.fori_loop(1, nwide, greet, 0)
    pl.semaphore_signal(barrier, inc=1, device_id=sibling, device_id_type=MESH)
    pl.semaphore_signal(barrier, inc=1, device_id=mate, device_id_type=MESH)

    key, weight = routing(ids_ref[...], probs_ref[...], slot_ref)
    loads[0].wait()
    loads[1].wait()

    def pick(kind):
        span = pl.ds(kind * per_kind, per_kind)
        slot = lax.broadcasted_iota(jnp.int32, (per_kind, rows), 0) % CAP
        chosen = jnp.where(dot(spread(kind, npair), key) == slot.astype(F32), 1.0, 0.0).astype(BF16)
        sel[span, :] = chosen
        picked[span, :] = dot(chosen, tok[...]).astype(BF16)

    pick(0)
    pick(2)
    pl.semaphore_wait(barrier, nwide + 1)

    def incoming(which, chip):
        return across(chip) if which == 0 else pl.ds(0, 2 * wblk)

    def send_kept(i, which, row):
        index = turn(i)
        device = peer(index)
        columns = incoming(which, device[1] // 2)
        remote(
            picked.at[pl.ds(pl.multiple_of(row(index), CAP), CAP), columns],
            block(recv_k.at[which, core], i).at[:, columns],
            dsend.at[which],
            drecv.at[which, i // group],
            device,
        ).start()

    def keep_kept(which, row):
        columns = incoming(which, x_lo)
        pltpu.make_async_copy(
            picked.at[pl.ds(pl.multiple_of(row(wide), CAP), CAP), columns],
            block(recv_k.at[which, core], 0).at[:, columns],
            drecv.at[which, 0],
        ).start()

    def row_0(index):
        to_owner = 1 - (index % 2 + index // 2) % 2
        return to_owner * (2 * per_kind) + index // 2 * CAP

    def send_0(i, carry):
        send_kept(i, 0, row_0)
        return carry

    lax.fori_loop(1, nwide, send_0, 0)
    keep_kept(0, row_0)

    pick(3)

    def piece_r(index):
        return picked.at[
            pl.ds(pl.multiple_of(3 * per_kind + index // 2 * CAP, CAP), CAP),
            pl.ds(pl.multiple_of(index % 2 * wblk, wblk), wblk),
        ]

    def send_r(i, carry):
        index = turn(i)
        remote(
            piece_r(index), block(recv_r.at[core], wide), dsend.at[2], drecv.at[2, 0], peer(index)
        ).start()
        return carry

    lax.fori_loop(1, nwide, send_r, 0)
    pltpu.make_async_copy(piece_r(wide), block(recv_r.at[core], wide), drecv.at[2, 0]).start()

    pick(1)

    def row_1(index):
        return per_kind + index // 2 * CAP

    def send_1(i, carry):
        index = turn(i)

        @pl.when((index % 2 + index // 2) % 2 == 1)
        def _():
            send_kept(i, 1, row_1)

        return carry

    lax.fori_loop(1, nwide, send_1, 0)

    @pl.when(owner == 0)
    def _():
        keep_kept(1, row_1)

    high = weight.astype(BF16)
    low = (weight - high.astype(F32)).astype(BF16)
    for part, value in enumerate((high, low)):
        for kind in range(4):
            span = pl.ds(kind * per_kind, per_kind)
            taken = sel[span, :].astype(F32) * dot(spread(kind, npair), value)
            coef[part * rows : (part + 1) * rows, span] = taken.T.astype(BF16)

    mine = pl.ds(pl.multiple_of(side * half, half), half)
    theirs = pl.ds(pl.multiple_of((1 - side) * half, half), half)
    forward = remote(recv_r.at[core], recv_r.at[core], fsend.at[2, 0, 0], frecv.at[2, 0, 0], sibling)
    swap = remote(part_out, part_in, psend.at[0], precv.at[0], partner)
    share = remote(hid_r.at[mine], hid_r.at[mine], psend.at[1], precv.at[1], partner)

    def fresh_partial():
        arrived(recv_r.at[core], drecv.at[2, 0])
        forward.start()
        loads[2].wait()
        depth = pl.ds(pl.multiple_of(core * wblk, wblk), wblk)
        for g in range(2):
            acc[g] = dot(recv_r[core], fi[g, depth, :])
        forward.wait_recv()
        depth = pl.ds(pl.multiple_of((1 - core) * wblk, wblk), wblk)
        for g in range(2):
            acc[g] += dot(recv_r[1 - core], fi[g, depth, :])
        for g in range(2):
            part_out[g] = acc[g, theirs, :].astype(BF16)
            part_own[g] = acc[g, mine, :]
        swap.start()

    def fresh_hidden():
        swap.wait_recv()
        hid_r[mine, :] = gated(
            part_own[0] + part_in[0].astype(F32), part_own[1] + part_in[1].astype(F32)
        )
        share.start()

    def give(which, part, t, source, target, span):
        return remote(
            source.at[:, span],
            target.at[:, span],
            osend.at[which, part, t],
            orecv.at[which, part, t],
            sibling,
        )

    def fresh_down_and_back():
        loads[3].wait()
        forward.wait_send()
        arrived(hid_r.at[theirs], precv.at[1])
        given = []
        for t in range(2):
            span = pl.ds(t * tile, tile)
            columns = pl.ds(pl.multiple_of((1 - core) * wblk + t * tile, tile), tile)
            recv_r[1 - core, :, span] = dot(hid_r[...], fd[:, columns]).astype(BF16)
            given.append(give(2, 0, t, recv_r.at[1 - core], in_r, span))
            given[t].start()
        for t in range(2):
            span = pl.ds(t * tile, tile)
            columns = pl.ds(pl.multiple_of(core * wblk + t * tile, tile), tile)
            given[t].wait_recv()
            recv_r[core, :, span] = (
                dot(hid_r[...], fd[:, columns]) + in_r[:, span].astype(F32)
            ).astype(BF16)
        slot = ret.at[
            pl.ds(pl.multiple_of(3 * per_kind + pair * CAP, CAP), CAP),
            pl.ds(pl.multiple_of(side * wblk, wblk), wblk),
        ]

        def back(i, carry):
            index = turn(i)
            remote(
                block(recv_r.at[core], index), slot, rsend.at[2], rrecv.at[3], peer(index)
            ).start()
            return carry

        lax.fori_loop(1, nwide, back, 0)
        pltpu.make_async_copy(block(recv_r.at[core], wide), slot, rrecv.at[3]).start()
        for copy in given:
            copy.wait_send()

    unchanged = (slot_ref[pair] + 1) % 2
    far = alone(1 - x_lo)

    def rows_of(which, g, columns, where=core):
        return recv_k.at[which, where, pl.ds(g * span_g, span_g), columns]

    def forward_near(which, g):
        ref = rows_of(which, g, incoming(which, x_lo))
        return remote(ref, ref, fsend.at[which, g, 0], frecv.at[which, g, 0], sibling)

    def forward_far(which, g):
        ref = rows_of(which, g, far)
        return remote(ref, ref, fsend.at[which, g, 1], frecv.at[which, g, 1], sibling)

    def lend(which, g):
        ref = rows_of(which, g, alone(x_lo))
        return remote(ref, ref, csend.at[which, g], crecv.at[which, g], mate)

    def relay(which, g):
        arrived(rows_of(which, g, incoming(which, x_lo)), drecv.at[which, g])
        if which == 0:
            lend(which, g).start()
        forward_near(which, g).start()

    def relay_far(which, g):
        arrived(rows_of(which, g, far), crecv.at[which, g])
        forward_far(which, g).start()

    def alone_at(where, chip):
        return chip * direct, (where + 2 * chip) * wblk + chip * common

    def common_at(where):
        return (lone, where * wblk + lone), (wblk, (where + 2) * wblk)

    def half_of(part):
        return pl.ds(part * half, half)

    def groups_of(part):
        return range(part * GROUPS // HALVES, (part + 1) * GROUPS // HALVES)

    def gate_and_up(which, part, expert):
        here = half_of(part)

        def multiply(where, offset, row, size, first=False):
            offset, row = pl.multiple_of(offset, 128), pl.multiple_of(row, 128)
            for g in range(2):
                term = dot(
                    recv_k[which, where, here, pl.ds(offset, size)],
                    wi[expert, g, pl.ds(row, size), :],
                )
                if first:
                    acc[g, here, :] = term
                else:
                    acc[g, here, :] += term

        def multiply_alone(where, chip, first=False):
            multiply(where, *alone_at(where, chip), lone, first)

        def multiply_common(where):
            for place in common_at(where):
                multiply(where, *place, common)

        if which == 0:
            multiply_alone(core, x_lo, True)
            multiply_common(core)
            multiply_alone(core, 1 - x_lo)
        else:
            multiply(core, 0, core * wblk, wblk, True)
            multiply(core, wblk, (core + 2) * wblk, wblk)
        for g in groups_of(part):
            forward_near(which, g).wait_recv()
        if which == 0:
            multiply_alone(1 - core, x_lo)
            multiply_common(1 - core)
            for g in groups_of(part):
                forward_far(which, g).wait_recv()
            multiply_alone(1 - core, 1 - x_lo)
        else:
            multiply(1 - core, 0, (1 - core) * wblk, wblk)
            multiply(1 - core, wblk, (3 - core) * wblk, wblk)
        hid[here, :] = gated(acc[0, here, :], acc[1, here, :])

    def tiles_at(where):
        return (
            (*alone_at(where, 1 - x_lo), lone),
            (*alone_at(where, x_lo), lone),
            *((*place, common) for place in common_at(where)),
        )

    def give_tile(which, part, t):
        offset, _, size = tiles_at(core)[t]
        here = half_of(part)
        return give(
            which,
            part,
            t,
            recv_k.at[which, 1 - core, here],
            in_k.at[which, here],
            pl.ds(pl.multiple_of(offset, 128), size),
        )

    def cross(which, part):
        here = half_of(part)
        return remote(
            recv_k.at[which, core, here, far],
            in_x.at[which, here],
            xsend.at[which, part],
            xrecv.at[which, part],
            mate,
        )

    def send_back(which, part, kind, columns):
        slot = ret.at[pl.ds(pl.multiple_of(kind * per_kind + pair * CAP, CAP), CAP), columns]

        def back(i, carry):
            remote(
                block(recv_k.at[which, core], i).at[:, columns],
                slot,
                rsend.at[which],
                rrecv.at[kind],
                peer(turn(i, -1)),
            ).start()
            return carry

        each = nwide // HALVES
        lax.fori_loop(max(1, part * each), (part + 1) * each, back, 0)
        if part == 0:
            pltpu.make_async_copy(
                block(recv_k.at[which, core], 0).at[:, columns], slot, rrecv.at[kind]
            ).start()

    def down(which, part, expert, kind):
        here = half_of(part)
        for g in groups_of(part):
            forward_near(which, g).wait_send()
            if which == 0:
                lend(which, g).wait_send()
                forward_far(which, g).wait_send()
        for t, (offset, column, size) in enumerate(tiles_at(1 - core)):
            span = pl.ds(pl.multiple_of(offset, 128), size)
            columns = pl.ds(pl.multiple_of(column, 128), size)
            recv_k[which, 1 - core, here, span] = dot(
                hid[here, :], wd[expert, :, columns]
            ).astype(BF16)
            give_tile(which, part, t).start()

        def own_tile(t):
            offset, column, size = tiles_at(core)[t]
            span = pl.ds(pl.multiple_of(offset, 128), size)
            columns = pl.ds(pl.multiple_of(column, 128), size)
            give_tile(which, part, t).wait_recv()
            recv_k[which, core, here, span] = (
                dot(hid[here, :], wd[expert, :, columns]) + in_k[which, here, span].astype(F32)
            ).astype(BF16)

        own_tile(0)
        cross(which, part).start()
        own_tile(2)
        own_tile(3)
        send_back(which, part, kind, pl.ds(lone, 2 * common))
        own_tile(1)

    def finish(which, part, kind):
        here = half_of(part)
        cross(which, part).wait_recv()
        lot = alone(x_lo)
        recv_k[which, core, here, lot] = (
            recv_k[which, core, here, lot].astype(F32) + in_x[which, here].astype(F32)
        ).astype(BF16)
        send_back(which, part, kind, lot)

    def settle(which):
        for part in range(HALVES):
            cross(which, part).wait_send()
            for t in range(4):
                give_tile(which, part, t).wait_send()

    first_expert = owner * unchanged
    first_kind = owner * 2
    for g in range(GROUPS):
        relay(0, g)
        if g > 0:
            relay_far(0, g - 1)
    loads[4].wait()
    loads[5].wait()
    gate_and_up(0, 0, first_expert)
    relay_far(0, GROUPS - 1)
    down(0, 0, first_expert, first_kind)
    gate_and_up(0, 1, first_expert)
    down(0, 1, first_expert, first_kind)
    fresh_partial()
    finish(0, 0, first_kind)

    @pl.when(owner == 0)
    def _():
        relay(1, 0)
        relay(1, 1)

    finish(0, 1, first_kind)

    @pl.when(owner == 0)
    def _():
        gate_and_up(1, 0, 1)
        down(1, 0, 1, 1)
        for g in range(2, GROUPS):
            relay(1, g)
        gate_and_up(1, 1, 1)
        down(1, 1, 1, 1)

    @pl.when(owner == 0)
    def _():
        finish(1, 0, 1)

    fresh_hidden()
    fresh_down_and_back()

    @pl.when(owner == 0)
    def _():
        finish(1, 1, 1)
        settle(1)

    settle(0)

    for kind in (0, 2, 3, 1):
        span = pl.ds(kind * per_kind, per_kind)
        if kind == 3:
            arrived(ret.at[span], rrecv.at[kind])
        else:
            arrived(ret.at[span, across(x_lo)], rrecv.at[kind])
        for chip in range(2):
            columns = pl.ds(pl.multiple_of((x_lo + 1 - chip) % 2 * wblk, wblk), wblk)
            both = dot(coef[:, span], ret[span, columns])
            if kind == 0:
                mixing[chip] = both[:rows] + both[rows:]
            else:
                mixing[chip] += both[:rows] + both[rows:]
    mix_out[...] = mixing[0].astype(BF16)
    last = remote(mix_out, mix_in, psend.at[2], precv.at[2], mate)
    last.start()
    last.wait_recv()
    out_ref[...] = (mixing[1] + mix_in[...].astype(F32)).astype(BF16)

    swap.wait_send()
    share.wait_send()
    last.wait_send()
    sent = total - CAP
    arrived(recv_r.at[0, pl.ds(0, sent)], dsend.at[2])
    arrived(recv_r.at[0, pl.ds(0, sent)], rsend.at[2])
    arrived(recv_k.at[0, 0, pl.ds(0, sent), :direct], dsend.at[0])
    arrived(recv_k.at[0, 0, pl.ds(0, sent), :direct], rsend.at[0])

    @pl.when(owner == 1)
    def _():
        arrived(recv_k.at[0, 0, pl.ds(0, per_kind)], dsend.at[1])

    @pl.when(owner == 0)
    def _():
        arrived(recv_k.at[0, 0, pl.ds(0, per_kind - CAP)], dsend.at[1])
        arrived(recv_k.at[0, 0, pl.ds(0, sent), :direct], rsend.at[1])


def on_device(nwide, tokens, expert_ids, probs, w_in, w_down, fresh_in, fresh_down, refresh_slot):
    rows, width = tokens.shape
    units = w_down.shape[1]
    wblk = width // 4
    total = nwide * CAP
    slots = 2 * total
    dma = pltpu.SemaphoreType.DMA
    hbm = pl.BlockSpec(memory_space=pl.ANY)
    vmem = pl.BlockSpec(memory_space=pltpu.VMEM)
    return pl.pallas_call(
        functools.partial(kernel, nwide),
        out_shape=jax.ShapeDtypeStruct((rows, wblk), BF16),
        in_specs=[hbm, vmem, vmem, pl.BlockSpec(memory_space=pltpu.SMEM), hbm, hbm, hbm, hbm],
        out_specs=vmem,
        scratch_shapes=[
            pltpu.VMEM((rows, 2 * wblk), BF16),
            pltpu.VMEM((slots, rows), BF16),
            pltpu.VMEM((2 * rows, slots), BF16),
            pltpu.VMEM((slots, 2 * wblk), BF16),
            pltpu.VMEM((2, total, wblk), BF16),
            pltpu.VMEM((2, 2, total, 2 * wblk), BF16),
            pltpu.VMEM(w_in.shape, BF16),
            pltpu.VMEM(w_down.shape, BF16),
            pltpu.VMEM(fresh_in.shape, BF16),
            pltpu.VMEM(fresh_down.shape, BF16),
            pltpu.VMEM((2, total, units), F32),
            pltpu.VMEM((total, units), BF16),
            pltpu.VMEM((total, units), BF16),
            pltpu.VMEM((2, total // 2, units), BF16),
            pltpu.VMEM((2, total // 2, units), BF16),
            pltpu.VMEM((2, total // 2, units), F32),
            pltpu.VMEM((total, wblk), BF16),
            pltpu.VMEM((2, total, 2 * wblk), BF16),
            pltpu.VMEM((2, total, wblk * 7 // 8), BF16),
            pltpu.VMEM((slots, 2 * wblk), BF16),
            pltpu.VMEM((2, rows, wblk), F32),
            pltpu.VMEM((rows, wblk), BF16),
            pltpu.VMEM((rows, wblk), BF16),
            dma((6,)),
            dma((3,)),
            dma((3, GROUPS)),
            dma((3, GROUPS, 2)),
            dma((3, GROUPS, 2)),
            dma((2, GROUPS)),
            dma((2, GROUPS)),
            dma((2, HALVES)),
            dma((2, HALVES)),
            dma((3, HALVES, 4)),
            dma((3, HALVES, 4)),
            dma((3,)),
            dma((3,)),
            dma((3,)),
            dma((4,)),
        ],
        compiler_params=pltpu.CompilerParams(
            collective_id=0, has_side_effects=True, vmem_limit_bytes=63 * 1024 * 1024
        ),
    )(tokens, expert_ids.T, probs.T, refresh_slot, w_in, w_down, fresh_in, fresh_down)


def solution(mesh):
    return jax.shard_map(
        functools.partial(on_device, mesh.shape["wide"]),
        mesh=mesh,
        in_specs=(
            P("wide", None),
            P("wide", None),
            P("wide", None),
            P("wide", None, None, "narrow"),
            P("wide", "narrow", None),
            P(None, "wide", "narrow"),
            P("narrow", "wide"),
            P(),
        ),
        out_specs=P("wide", "narrow"),
        check_vma=False,
    )
```
